128 devices in a mesh: pp: 8 (over y, core), ep: 16 (over z, x).
Axes of the slice: x: 4, y: 4, z: 4, core: 2. Of those that a mesh axis runs over, the one named last changes fastest.
Arguments:
- forward_acts: bfloat16 [8, 2048, 3584], P('pp', 'ep'), may hold values from -6 to 6
- forward_ids: int32 [8, 2048, 2], P('pp', 'ep'), may hold values from 0 to 15, all different within a row; in each aligned block of 128 rows (0 to 127, 128 to 255, ..., all dimensions but the last counted through in order) at most 24 rows name the same one
- backward_acts: bfloat16 [8, 2048, 3584], P('pp', 'ep'), may hold values from -6 to 6
- backward_ids: int32 [8, 2048, 2], P('pp', 'ep'), may hold values from 0 to 15, all different within a row; in each aligned block of 128 rows (0 to 127, 128 to 255, ..., all dimensions but the last counted through in order) at most 24 rows name the same one
- upstream_grad: bfloat16 [8, 2048, 3584], P('pp', 'ep'), may hold values from -6 to 6
- gate_up_weight: bfloat16 [8, 16, 3584, 2048], P('pp', 'ep'), may hold values from -0.09375 to 0.09375
- down_weight: bfloat16 [8, 16, 1024, 3584], P('pp', 'ep'), may hold values from -0.1875 to 0.1875
- router_weight: bfloat16 [8, 3584, 16], P('pp'), may hold values from -0.09375 to 0.09375
- mirror_grads: float32 [8, 3584, 16], P('pp', 'ep'), may hold values from -6 to 6
Outputs:
- next_acts: bfloat16 [8, 2048, 3584], P('pp', 'ep')
- next_grads: bfloat16 [8, 2048, 3584], P('pp', 'ep')
- router_grads: float32 [8, 3584, 16], P('pp', 'ep')
The draws below stay inside these ranges and needn't reach their ends.
Inputs may be any that keep to these rules, and one draw needn't show every extreme that they name: `forward_ids`: each token names 2 different experts. Among the 128 tokens of one device, no expert is named more than 24 times. `backward_ids`: as for forward_ids.
All inputs are finite; a program needn't handle non-finite values.
Results may differ from the reference program's by a relative error of at most 0.015.
Values may be sent and summed in bfloat16 or wider, within the bound.
No kernel may reach another device: no remote copies, remote signals or barrier semaphores. Data moves between devices by JAX's collectives and lax.ppermute only.
A program may use at most 128 MiB of HBM per device.

```python
import math
import jax
import jax.numpy as jnp
import numpy as np
from jax import lax

D = 3584
HID = 1024
TOK_DEV = 128
TOPK = 2
EXPERTS = 16
CAP = 24
TOKENS = 2048
N_PP = 8
N_EP = 16


def with_spikes(drawn, own_key, source, target, blocks, factor):
    def block_of(position):
        return (jnp.arange(drawn.shape[position]) // (drawn.shape[position] // blocks)).reshape((-1,) + (1,) * (drawn.ndim - 1 - position))

    one_side = jax.random.permutation(own_key, blocks)[block_of(target)]
    far = (block_of(target) + blocks // 2) % blocks
    return jnp.where((block_of(source) == one_side) | (block_of(source) == far), factor * drawn, drawn)


def block_scale(own_key, shape, pieces, smallest, top_value):
    gain = 1.0
    for position, parts in pieces:
        steps = jax.random.uniform(jax.random.fold_in(jax.random.fold_in(own_key, 6), position), (parts,), jnp.float32, smallest / len(pieces), top_value / len(pieces))
        gain = gain * jnp.repeat(jnp.exp(steps), shape[position] // parts).reshape((-1,) + (1,) * (len(shape) - 1 - position))
    return gain


def assign_block(key, own, number, rows, count, top, bound, lean):
    sequence = jax.random.permutation(key, count)
    heavy_load, usual = shares(count, rows * top, bound, lean, True), shares(count, rows * top, bound, lean, False)
    places = jnp.arange(count)

    def named(tallies, offset_by):
        used = int((tallies > 0).sum())
        fixed = max(1, used // 4)
        moved = fixed + (places - fixed + offset_by * (used - fixed)) % max(1, count - fixed)
        return jnp.zeros((count,), jnp.int32).at[sequence[jnp.where(places < fixed, places, moved)]].set(jnp.asarray(tallies, jnp.int32))

    tallies = jnp.where(number % 4 == 0, named(heavy_load, number // 4), named(usual, number - number // 4 - 1))
    mixed = jax.random.permutation(jax.random.fold_in(own, 3), count)
    giver, sink = mixed[0:count // 2 * 2:2], mixed[1:count // 2 * 2:2]
    margin = jnp.minimum(tallies[giver] - 1, bound - tallies[sink]) // 2
    margin = jnp.where((giver == sequence[0]) | (sink == sequence[0]) | (tallies[sink] == 0), 0, jnp.maximum(margin, 0))
    moved = jax.random.randint(jax.random.fold_in(own, 4), (count // 2,), 0, 1 << 20) % (margin + 1)
    tallies = tallies.at[giver].add(-moved).at[sink].add(moved)
    items = jnp.searchsorted(jnp.cumsum(tallies), jnp.arange(rows * top), side="right").astype(jnp.int32)
    table = items.reshape(top, rows).T
    table = table[jax.random.permutation(jax.random.fold_in(own, 1), rows)]
    offset_by = jax.random.randint(jax.random.fold_in(own, 2), (rows, 1), 0, top)
    return jnp.take_along_axis(table, (jnp.arange(top)[None, :] + offset_by) % top, axis=1)


def shares(number_of, total, limit, skew, full):
    loads = [(1 << 20) // math.isqrt(grade ** skew) + 1 for grade in range(1, number_of + 1)]
    largest = limit if full else min(limit, max(-(-total // number_of), total * loads[0] // sum(loads)))
    least = 1 if total - largest >= number_of - 1 else 0
    counts, rest = [largest] + [least] * (number_of - 1), total - largest - least * (number_of - 1)
    while rest > 0:
        free = [i for i in range(1, number_of) if counts[i] < largest] or [i for i in range(1, number_of) if counts[i] < limit]
        mass, budget = sum([loads[i] for i in free]), rest
        for i in free:
            more = min(limit - counts[i], max(1, budget * loads[i] // mass), rest)
            counts[i] = counts[i] + more
            rest = rest - more
    return np.array(counts)


def gaussian(stream_key, dims, spread, reach, split=(), held_as=jnp.bfloat16):
    values = jax.random.normal(stream_key, dims, jnp.float32) * spread
    if len(split) > 0:
        values = block_scale(stream_key, dims, split, -0.22, 0.18) * values
    return jnp.clip(values, min=-reach, max=reach).astype(held_as)


def bell_draw_with(key, extent, spread, bound, cuts, heavy, kind=jnp.bfloat16):
    values = spread * jax.random.normal(key, extent, jnp.float32)
    if cuts:
        values = values * block_scale(key, extent, cuts, -0.22, 0.18)
    return jnp.clip(with_spikes(values, jax.random.fold_in(key, 3), *heavy), -bound, bound).astype(kind)


def setup_inputs(seed: int = 0) -> dict:
    key_list = jax.random.split(jax.random.key(seed), 10)
    forward_acts = gaussian(key_list[0], (N_PP, TOKENS, D), 1.0, 6.0, ((0, 8), (1, 16)))
    forward_ids_keys = jax.random.split(jax.random.fold_in(key_list[1], 1), N_PP * TOKENS // TOK_DEV)
    forward_ids_turns = jax.random.permutation(jax.random.fold_in(key_list[1], 3), N_PP * TOKENS // TOK_DEV)
    forward_ids = jax.vmap(lambda own, number: assign_block(jax.random.fold_in(key_list[1], 2), own, number, TOK_DEV, EXPERTS, TOPK, CAP, 2))(forward_ids_keys, forward_ids_turns).reshape((N_PP, TOKENS, TOPK))
    backward_acts = bell_draw_with(key_list[2], (N_PP, TOKENS, D), 1.0, 6.0, ((0, 8), (1, 16)), (1, 2, 16, 2.0))
    backward_ids_keys = jax.random.split(jax.random.fold_in(key_list[3], 1), N_PP * TOKENS // TOK_DEV)
    backward_ids_turns = jax.random.permutation(jax.random.fold_in(key_list[3], 3), N_PP * TOKENS // TOK_DEV)
    backward_ids = jax.vmap(lambda own, number: assign_block(jax.random.fold_in(key_list[3], 2), own, number, TOK_DEV, EXPERTS, TOPK, CAP, 2))(backward_ids_keys, backward_ids_turns).reshape((N_PP, TOKENS, TOPK))
    upstream_grad = gaussian(key_list[4], (N_PP, TOKENS, D), 1.0, 6.0, ((0, 8), (1, 16)))
    gate_up_weight = gaussian(key_list[5], (N_PP, EXPERTS, D, 2 * HID), D ** -0.5, 0.09375, ((0, 8), (1, 16)))
    down_weight = gaussian(key_list[6], (N_PP, EXPERTS, HID, D), HID ** -0.5, 0.1875, ((0, 8), (1, 16)))
    router_weight = gaussian(key_list[7], (N_PP, D, EXPERTS), D ** -0.5, 0.09375, ((0, 8),))
    mirror_grads = gaussian(key_list[8], (N_PP, D, EXPERTS), 1.0, 6.0, ((0, 8), (1, 16)), jnp.float32)
    return {"forward_acts": forward_acts, "forward_ids": forward_ids, "backward_acts": backward_acts, "backward_ids": backward_ids, "upstream_grad": upstream_grad, "gate_up_weight": gate_up_weight, "down_weight": down_weight, "router_weight": router_weight, "mirror_grads": mirror_grads}


def expert_forward(inputs, gate_up, down):
    joined = jnp.dot(inputs, gate_up, preferred_element_type=jnp.float32)
    width = down.shape[0]
    pre_gate = joined[:, :width]
    pre_up = joined[:, width:]
    hidden = (pre_gate * jax.nn.sigmoid(pre_gate) * pre_up).astype(jnp.bfloat16)
    return jnp.dot(hidden, down, preferred_element_type=jnp.float32).astype(jnp.bfloat16)


def expert_backward(inputs, upstream, gate_up, down):
    joined = jnp.dot(inputs, gate_up, preferred_element_type=jnp.float32)
    width = down.shape[0]
    pre_gate = joined[:, :width]
    pre_up = joined[:, width:]
    squash = jax.nn.sigmoid(pre_gate)
    swished = pre_gate * squash
    hidden = (swished * pre_up).astype(jnp.bfloat16)
    produced = jnp.dot(hidden, down, preferred_element_type=jnp.float32).astype(jnp.bfloat16)
    hidden_grad = lax.dot_general(upstream, down, (((1,), (1,)), ((), ())), preferred_element_type=jnp.float32)
    gate_part = hidden_grad * pre_up * squash * (1.0 + pre_gate * (1.0 - squash))
    up_part = hidden_grad * swished
    joined_grad = jnp.concatenate([gate_part, up_part], axis=1).astype(jnp.bfloat16)
    row_grad = lax.dot_general(joined_grad, gate_up, (((1,), (1,)), ((), ())), preferred_element_type=jnp.float32)
    return row_grad.astype(jnp.bfloat16), produced


def slot_table(ids):
    flat = ids.reshape(N_EP, TOK_DEV * TOPK).astype(jnp.int32)
    hot = (flat[:, :, None] == jnp.arange(EXPERTS, dtype=jnp.int32)[None, None, :]).astype(jnp.int32)
    before = jnp.sum((jnp.cumsum(hot, axis=1) - 1) * hot, axis=-1)
    slot_index = (jnp.arange(N_EP, dtype=jnp.int32)[:, None] * CAP + before).reshape(-1).astype(jnp.int32)
    experts_flat = ids.reshape(-1).astype(jnp.int32)
    row_count = experts_flat.shape[0]
    table = jnp.full((EXPERTS, N_EP * CAP), row_count, jnp.int32)
    table = table.at[experts_flat, slot_index].set(jnp.arange(row_count, dtype=jnp.int32))
    return experts_flat, slot_index, table


def gather_rows(tokens, table):
    padded = jnp.concatenate([jnp.repeat(tokens, TOPK, axis=0), jnp.zeros((1, tokens.shape[1]), tokens.dtype)], axis=0)
    return padded[table]


def gating(tokens, ids, router_section):
    logits = jnp.dot(tokens, router_section, preferred_element_type=jnp.float32)
    affinity = jax.nn.sigmoid(jnp.take_along_axis(logits, ids.astype(jnp.int32), axis=1))
    total = jnp.sum(affinity, axis=1, keepdims=True)
    return affinity, affinity / total, total


def one_section(section_args):
    acts_fwd, ids_fwd, acts_bwd, ids_bwd, upstream, gate_up, down, router_section = section_args
    count = acts_fwd.shape[0]
    width = acts_fwd.shape[1]
    _, gates_fwd, _ = gating(acts_fwd, ids_fwd, router_section)
    experts_fwd, slots_fwd, table_fwd = slot_table(ids_fwd)
    inputs_fwd = gather_rows(acts_fwd, table_fwd)
    outputs_fwd = lax.map(lambda item: expert_forward(item[0], item[1], item[2]), (inputs_fwd, gate_up, down))
    rows_fwd = outputs_fwd[experts_fwd, slots_fwd].reshape(count, TOPK, width).astype(jnp.float32)
    layer_out = (acts_fwd.astype(jnp.float32) + jnp.sum(gates_fwd[:, :, None] * rows_fwd, axis=1)).astype(jnp.bfloat16)

    affinity, gates_bwd, total = gating(acts_bwd, ids_bwd, router_section)
    experts_bwd, slots_bwd, table_bwd = slot_table(ids_bwd)
    inputs_bwd = gather_rows(acts_bwd, table_bwd)
    grads_in = gather_rows(upstream, table_bwd)
    row_grads, produced = lax.map(lambda item: expert_backward(item[0], item[1], item[2], item[3]), (inputs_bwd, grads_in, gate_up, down))
    grad_rows = row_grads[experts_bwd, slots_bwd].reshape(count, TOPK, width).astype(jnp.float32)
    out_rows = produced[experts_bwd, slots_bwd].reshape(count, TOPK, width).astype(jnp.float32)
    upstream_f = upstream.astype(jnp.float32)
    gate_grad = jnp.sum(upstream_f[:, None, :] * out_rows, axis=-1)
    mean_term = jnp.sum(gates_bwd * gate_grad, axis=1, keepdims=True)
    logit_rows = (gate_grad - mean_term) / total * affinity * (1.0 - affinity)
    expert_hot = (ids_bwd[:, :, None] == jnp.arange(EXPERTS, dtype=jnp.int32)[None, None, :]).astype(jnp.float32)
    logit_grad = jnp.sum(logit_rows[:, :, None] * expert_hot, axis=1)
    router_back = lax.dot_general(logit_grad, router_section.astype(jnp.float32), (((1,), (1,)), ((), ())), precision=lax.Precision.HIGHEST, preferred_element_type=jnp.float32)
    input_grad = (upstream_f + jnp.sum(gates_bwd[:, :, None] * grad_rows, axis=1) + router_back).astype(jnp.bfloat16)
    router_part = lax.dot_general(acts_bwd.astype(jnp.float32), logit_grad, (((0,), (0,)), ((), ())), precision=lax.Precision.HIGHEST, preferred_element_type=jnp.float32) / TOK_DEV
    return layer_out, input_grad, router_part


def reference(forward_acts, forward_ids, backward_acts, backward_ids, upstream_grad, gate_up_weight, down_weight, router_weight, mirror_grads):
    layer_out, input_grad, router_part = lax.map(one_section, (forward_acts, forward_ids, backward_acts, backward_ids, upstream_grad, gate_up_weight, down_weight, router_weight))
    next_acts = jnp.roll(layer_out, 1, axis=0)
    next_grads = jnp.roll(input_grad, -1, axis=0)
    router_grads = router_part + mirror_grads[::-1]
    return next_acts, next_grads, router_grads
```

```python
import jax
import jax.numpy as jnp
from jax import lax
from jax.sharding import PartitionSpec as P


def shifted(value, axis, steps):
    count = lax.axis_size(axis)
    pairs = [(source, (source + steps) % count) for source in range(count)]
    return lax.ppermute(value, axis, pairs)


def exchange(value):
    return lax.all_to_all(value, "ep", split_axis=0, concat_axis=0, tiled=True)


def after(value, *earlier):
    return lax.optimization_barrier((value, *earlier))[0]


def split_two(value):
    high = value.astype(jnp.bfloat16)
    low = (value - high.astype(jnp.float32)).astype(jnp.bfloat16)
    return high, low


def gating(tokens, ids, router_section):
    row_count, top_count = ids.shape
    expert_count = router_section.shape[1]
    logits = jnp.dot(tokens, router_section, preferred_element_type=jnp.float32)
    expert_hot = ids[:, :, None] == lax.broadcasted_iota(
        jnp.int32, (row_count, top_count, expert_count), 2
    )
    affinity = jax.nn.sigmoid(jnp.sum(jnp.where(expert_hot, logits[:, None, :], 0.0), axis=-1))
    total = jnp.sum(affinity, axis=1, keepdims=True)
    return affinity, affinity / total, total, expert_hot


def slots(ids, expert_count, capacity):
    row_count, top_count = ids.shape
    flat_hot = (
        ids.reshape(-1, 1) == lax.broadcasted_iota(jnp.int32, (row_count * top_count, expert_count), 1)
    ).astype(jnp.bfloat16)
    entries = row_count * top_count
    earlier = (
        lax.broadcasted_iota(jnp.int32, (entries, entries), 1)
        < lax.broadcasted_iota(jnp.int32, (entries, entries), 0)
    ).astype(jnp.bfloat16)
    counts = jnp.dot(earlier, flat_hot, preferred_element_type=jnp.float32)
    before = jnp.sum(counts * flat_hot.astype(jnp.float32), axis=1).astype(jnp.int32)
    slot_index = ids * capacity + before.reshape(row_count, top_count)
    return slot_index[:, :, None] == lax.broadcasted_iota(
        jnp.int32, (row_count, top_count, expert_count * capacity), 2
    )


def pick(slot_hot, values):
    picker = jnp.any(slot_hot, axis=1).astype(jnp.bfloat16)
    return lax.dot_general(
        picker, values, (((0,), (0,)), ((), ())), preferred_element_type=jnp.float32
    ).astype(jnp.bfloat16)


def mixer(slot_hot, gates):
    return jnp.sum(jnp.where(slot_hot, gates[:, :, None], 0.0), axis=1).astype(jnp.bfloat16)


def on_device(
    forward_acts,
    forward_ids,
    backward_acts,
    backward_ids,
    upstream_grad,
    gate_up_weight,
    down_weight,
    router_weight,
    mirror_grads,
):
    joined_weight = gate_up_weight[0, 0]
    proj_weight = down_weight[0, 0]
    router_section = router_weight[0]
    tokens_fwd = forward_acts[0]
    tokens_bwd = backward_acts[0]
    upstream = upstream_grad[0]
    row_count, width = tokens_fwd.shape
    top_count = forward_ids.shape[2]
    expert_count = router_section.shape[1]
    hidden_units = proj_weight.shape[0]
    ranks = lax.axis_size("ep")
    capacity = 3 * row_count * top_count // (2 * ranks)
    shard = width // ranks
    early = (3 * width // 4) // 128 * 128

    slots_bwd = slots(backward_ids[0], expert_count, capacity)
    sent_bwd = pick(slots_bwd, jnp.concatenate([tokens_bwd, upstream], axis=1))
    got_bwd = exchange(sent_bwd)

    slots_fwd = slots(forward_ids[0], expert_count, capacity)
    sent_fwd = pick(slots_fwd, tokens_fwd)
    got_fwd = exchange(after(sent_fwd, got_bwd))

    joined = jnp.dot(got_bwd[:, :width], joined_weight, preferred_element_type=jnp.float32)
    pre_gate = joined[:, :hidden_units]
    pre_up = joined[:, hidden_units:]
    squash = jax.nn.sigmoid(pre_gate)
    swished = pre_gate * squash
    hidden = (swished * pre_up).astype(jnp.bfloat16).astype(jnp.float32)
    hidden_grad = lax.dot_general(
        got_bwd[:, width:], proj_weight, (((1,), (1,)), ((), ())), preferred_element_type=jnp.float32
    )
    gate_high, gate_low = split_two(jnp.sum(hidden * hidden_grad, axis=1, keepdims=True))
    gate_part = hidden_grad * pre_up * squash * (1.0 + pre_gate * (1.0 - squash))
    up_part = hidden_grad * swished
    joined_grad = jnp.concatenate([gate_part, up_part], axis=1).astype(jnp.bfloat16)
    row_grad = lax.dot_general(
        joined_grad, joined_weight, (((1,), (1,)), ((), ())), preferred_element_type=jnp.float32
    ).astype(jnp.bfloat16)
    extra = jnp.concatenate(
        [gate_high, gate_low, jnp.zeros((row_grad.shape[0], 126), jnp.bfloat16)], axis=1
    )
    back = exchange(after(jnp.concatenate([row_grad, extra], axis=1), got_fwd))

    joined = jnp.dot(got_fwd, joined_weight, preferred_element_type=jnp.float32)
    pre_gate = joined[:, :hidden_units]
    pre_up = joined[:, hidden_units:]
    hidden_fwd = (pre_gate * jax.nn.sigmoid(pre_gate) * pre_up).astype(jnp.bfloat16)
    produced = jnp.dot(hidden_fwd, proj_weight, preferred_element_type=jnp.float32).astype(jnp.bfloat16)
    returned_early = exchange(after(produced[:, :early], back))

    affinity, gates_bwd, total, hot_bwd = gating(tokens_bwd, backward_ids[0], router_section)
    gate_rows = [
        jnp.dot(
            slots_bwd[:, k].astype(jnp.bfloat16), back[:, width:], preferred_element_type=jnp.float32
        )
        for k in range(top_count)
    ]
    gate_grad = jnp.stack([rows[:, 0] + rows[:, 1] for rows in gate_rows], axis=1)
    mean_term = jnp.sum(gates_bwd * gate_grad, axis=1, keepdims=True)
    logit_rows = (gate_grad - mean_term) / total * affinity * (1.0 - affinity)
    logit_grad = jnp.sum(jnp.where(hot_bwd, logit_rows[:, :, None], 0.0), axis=1)
    logit_pair = jnp.concatenate(split_two(logit_grad), axis=1)
    router_back = lax.dot_general(
        logit_pair,
        jnp.concatenate([router_section, router_section], axis=1),
        (((1,), (1,)), ((), ())),
        preferred_element_type=jnp.float32,
    )
    grad_mix = jnp.dot(
        mixer(slots_bwd, gates_bwd), back[:, :width], preferred_element_type=jnp.float32
    )
    input_grad = (upstream.astype(jnp.float32) + grad_mix + router_back).astype(jnp.bfloat16)
    next_grads = shifted(input_grad, "pp", -1)

    router_pair = lax.dot_general(
        logit_pair, tokens_bwd, (((0,), (0,)), ((), ())), preferred_element_type=jnp.float32
    )
    router_part = ((router_pair[:expert_count] + router_pair[expert_count:]) / row_count).astype(
        jnp.bfloat16
    )
    wide = -(-shard // 128) * 128
    router_blocks = jnp.pad(
        router_part.reshape(expert_count, ranks, shard).transpose(1, 0, 2),
        ((0, 0), (0, capacity - expert_count), (0, wide - shard)),
    ).reshape(ranks * capacity, wide)

    late = jnp.concatenate([produced[:, early:], router_blocks], axis=1)
    returned_late = exchange(after(late, returned_early))

    _, gates_fwd, _, _ = gating(tokens_fwd, forward_ids[0], router_section)
    mixer_fwd = mixer(slots_fwd, gates_fwd)

    def finish(columns, rows):
        mixed = jnp.dot(mixer_fwd, rows, preferred_element_type=jnp.float32)
        return shifted((columns.astype(jnp.float32) + mixed).astype(jnp.bfloat16), "pp", 1)

    next_acts = jnp.concatenate(
        [
            finish(tokens_fwd[:, :early], returned_early),
            finish(tokens_fwd[:, early:], returned_late[:, : width - early]),
        ],
        axis=1,
    )

    count = lax.axis_size("pp")
    mirrored = lax.ppermute(mirror_grads[0], "pp", [(i, count - 1 - i) for i in range(count)])
    summed = jnp.sum(
        returned_late[:, width - early :]
        .reshape(ranks, capacity, wide)[:, :expert_count, :shard]
        .astype(jnp.float32),
        axis=0,
    )
    router_grads = summed.T + mirrored
    return (next_acts[None], next_grads[None], router_grads[None])


def solution(mesh):
    placed = (
        P("pp", "ep", None),
        P("pp", "ep", None),
        P("pp", "ep", None),
        P("pp", "ep", None),
        P("pp", "ep", None),
        P("pp", "ep", None, None),
        P("pp", "ep", None, None),
        P("pp", None, None),
        P("pp", "ep", None),
    )
    return jax.shard_map(
        on_device,
        mesh=mesh,
        in_specs=placed,
        out_specs=(P("pp", "ep", None), P("pp", "ep", None), P("pp", "ep", None)),
        check_vma=False,
    )
```

```python
import functools

import jax
import jax.numpy as jnp
from jax import lax
from jax.experimental import pallas as pl
from jax.experimental.pallas import tpu as pltpu
from jax.sharding import PartitionSpec as P

LANES = 128
BF16 = jnp.bfloat16
F32 = jnp.float32


def shifted(value, steps):
    count = lax.axis_size("pp")
    pairs = [(source, (source + steps) % count) for source in range(count)]
    return lax.ppermute(value, "pp", pairs)


def exchange(value):
    return lax.all_to_all(value, "ep", split_axis=0, concat_axis=0, tiled=True)


def split_two(value):
    high = value.astype(BF16)
    low = (value - high.astype(F32)).astype(BF16)
    return high, low


def call(kernel, grid, in_specs, out_specs, out_shape, scratch=(), aliases=None):
    return pl.pallas_call(
        kernel,
        grid=grid,
        in_specs=in_specs,
        out_specs=out_specs,
        out_shape=out_shape,
        scratch_shapes=scratch,
        input_output_aliases=aliases or {},
        compiler_params=pltpu.CompilerParams(vmem_limit_bytes=48 * 1024 * 1024),
        cost_estimate=pl.CostEstimate(flops=1000, bytes_accessed=1000, transcendentals=0),
    )


def slot_rows(ids, expert_count, capacity):
    top_count, tokens = ids.shape
    earlier = (
        lax.broadcasted_iota(jnp.int32, (tokens, tokens), 0)
        < lax.broadcasted_iota(jnp.int32, (tokens, tokens), 1)
    ).astype(F32)
    experts = lax.broadcasted_iota(jnp.int32, (expert_count, tokens), 0)
    taken = jnp.zeros((expert_count, 1), F32)
    rows = []
    for k in range(top_count):
        row = ids[k : k + 1]
        hot = (experts == row).astype(F32)
        before = jnp.dot(hot, earlier, preferred_element_type=F32) + taken
        taken = taken + jnp.sum(hot, axis=1, keepdims=True)
        place = jnp.sum(before * hot, axis=0, keepdims=True)
        rows.append(row * capacity + place.astype(jnp.int32))
    return rows


def picker_of(rows, slot_count):
    tokens = rows[0].shape[1]
    places = lax.broadcasted_iota(jnp.int32, (slot_count, tokens), 0)
    chosen = functools.reduce(jnp.logical_or, [places == row for row in rows])
    return chosen.astype(F32).astype(BF16)


def dispatch_kernel(
    sizes, ids_bwd, ids_fwd, acts_bwd, upstream, acts_fwd, sent_bwd, sent_fwd, slots, picker
):
    steps, expert_count, capacity = sizes
    step = pl.program_id(0)
    slot_count = expert_count * capacity

    @pl.when(step == 0)
    def _():
        rows_bwd = slot_rows(ids_bwd[...], expert_count, capacity)
        rows_fwd = slot_rows(ids_fwd[...], expert_count, capacity)
        picker[0] = picker_of(rows_bwd, slot_count)
        picker[1] = picker_of(rows_fwd, slot_count)
        slots[...] = jnp.concatenate(rows_bwd + rows_fwd, axis=0)

    @pl.when(step < steps)
    def _():
        sent_bwd[...] = jnp.dot(picker[0], acts_bwd[...], preferred_element_type=F32).astype(BF16)

    @pl.when(jnp.logical_and(step >= steps, step < 2 * steps))
    def _():
        sent_bwd[...] = jnp.dot(picker[0], upstream[...], preferred_element_type=F32).astype(BF16)

    @pl.when(step >= 2 * steps)
    def _():
        sent_fwd[...] = jnp.dot(picker[1], acts_fwd[...], preferred_element_type=F32).astype(BF16)


def dispatch(ids_bwd, ids_fwd, acts_bwd, upstream, acts_fwd, expert_count, capacity):
    tokens, width = acts_bwd.shape
    top_count = ids_bwd.shape[0]
    slot_count = expert_count * capacity
    steps = 2
    block = width // steps

    def part(number):
        return pl.BlockSpec(
            (tokens, block), lambda i: (0, jnp.clip(i - number * steps, 0, steps - 1))
        )

    whole = pl.BlockSpec((top_count, tokens), lambda i: (0, 0))
    return call(
        functools.partial(dispatch_kernel, (steps, expert_count, capacity)),
        (3 * steps,),
        [whole, whole, part(0), part(1), part(2)],
        [
            pl.BlockSpec((slot_count, block), lambda i: (0, jnp.minimum(i, 2 * steps - 1))),
            pl.BlockSpec((slot_count, block), lambda i: (0, jnp.clip(i - 2 * steps, 0, steps - 1))),
            pl.BlockSpec((2 * top_count, tokens), lambda i: (0, 0)),
        ],
        [
            jax.ShapeDtypeStruct((slot_count, 2 * width), BF16),
            jax.ShapeDtypeStruct((slot_count, width), BF16),
            jax.ShapeDtypeStruct((2 * top_count, tokens), jnp.int32),
        ],
        [pltpu.VMEM((2, slot_count, tokens), BF16)],
    )(ids_bwd, ids_fwd, acts_bwd, upstream, acts_fwd)


def backward_hidden_kernel(acts, grads, gate_w, up_w, down_w, gate_out, up_out, dots):
    pre_gate = jnp.dot(acts[...], gate_w[...], preferred_element_type=F32)
    pre_up = jnp.dot(acts[...], up_w[...], preferred_element_type=F32)
    hidden_grad = lax.dot_general(
        grads[...], down_w[...], (((1,), (1,)), ((), ())), preferred_element_type=F32
    )
    squash = jax.nn.sigmoid(pre_gate)
    swished = pre_gate * squash
    hidden = (swished * pre_up).astype(BF16).astype(F32)
    gate_out[...] = (
        hidden_grad * pre_up * squash * (1.0 + pre_gate * (1.0 - squash))
    ).astype(BF16)
    up_out[...] = (hidden_grad * swished).astype(BF16)

    @pl.when(pl.program_id(0) == 0)
    def _():
        dots[...] = jnp.zeros_like(dots)

    dots[...] += jnp.sum(hidden * hidden_grad, axis=1, keepdims=True)


def backward_hidden(got, joined_weight, proj_weight):
    slot_count = got.shape[0]
    width = got.shape[1] // 2
    hidden_units = proj_weight.shape[0]
    block = 256
    count = hidden_units // block
    return call(
        backward_hidden_kernel,
        (count,),
        [
            pl.BlockSpec((slot_count, width), lambda j: (0, 0), pipeline_mode=pl.Buffered(1)),
            pl.BlockSpec((slot_count, width), lambda j: (0, 1), pipeline_mode=pl.Buffered(1)),
            pl.BlockSpec((width, block), lambda j: (0, j)),
            pl.BlockSpec((width, block), lambda j: (0, count + j)),
            pl.BlockSpec((block, width), lambda j: (j, 0)),
        ],
        [
            pl.BlockSpec((slot_count, block), lambda j: (0, j)),
            pl.BlockSpec((slot_count, block), lambda j: (0, j)),
            pl.BlockSpec((slot_count, LANES), lambda j: (0, 0)),
        ],
        [
            jax.ShapeDtypeStruct((slot_count, hidden_units), BF16),
            jax.ShapeDtypeStruct((slot_count, hidden_units), BF16),
            jax.ShapeDtypeStruct((slot_count, LANES), F32),
        ],
    )(got, got, joined_weight, joined_weight, proj_weight)


def row_grad_kernel(block, gate_grad, up_grad, weight, dots, out):
    step = pl.program_id(0)
    units = gate_grad.shape[1]
    contract = (((1,), (1,)), ((), ()))
    rows = lax.dot_general(
        gate_grad[...], weight[:, :units], contract, preferred_element_type=F32
    ) + lax.dot_general(up_grad[...], weight[:, units:], contract, preferred_element_type=F32)
    out[:, pl.ds(pl.multiple_of(step * block, block), block)] = rows.astype(BF16)

    @pl.when(step == 0)
    def _():
        high, low = split_two(dots[...])
        lane = lax.broadcasted_iota(jnp.int32, dots.shape, 1)
        extra = jnp.where(lane == 0, high.astype(F32), jnp.where(lane == 1, low.astype(F32), 0.0))
        out[:, out.shape[1] - LANES :] = extra.astype(BF16)


def row_gradient(gate_grad, up_grad, joined_weight, dots):
    slot_count, units = gate_grad.shape
    width = joined_weight.shape[0]
    block = 512
    whole = pl.BlockSpec((slot_count, units), lambda j: (0, 0))
    return call(
        functools.partial(row_grad_kernel, block),
        (width // block,),
        [
            whole,
            whole,
            pl.BlockSpec((block, 2 * units), lambda j: (j, 0)),
            pl.BlockSpec((slot_count, LANES), lambda j: (0, 0)),
        ],
        pl.BlockSpec((slot_count, width + LANES), lambda j: (0, 0)),
        jax.ShapeDtypeStruct((slot_count, width + LANES), BF16),
    )(gate_grad, up_grad, joined_weight, dots)


def forward_hidden_kernel(acts, gate_w, up_w, out):
    pre_gate = jnp.dot(acts[...], gate_w[...], preferred_element_type=F32)
    pre_up = jnp.dot(acts[...], up_w[...], preferred_element_type=F32)
    out[...] = (pre_gate * jax.nn.sigmoid(pre_gate) * pre_up).astype(BF16)


def forward_hidden(got, joined_weight):
    slot_count, width = got.shape
    hidden_units = joined_weight.shape[1] // 2
    block = 256
    count = hidden_units // block
    return call(
        forward_hidden_kernel,
        (count,),
        [
            pl.BlockSpec((slot_count, width), lambda j: (0, 0), pipeline_mode=pl.Buffered(1)),
            pl.BlockSpec((width, block), lambda j: (0, j)),
            pl.BlockSpec((width, block), lambda j: (0, count + j)),
        ],
        pl.BlockSpec((slot_count, block), lambda j: (0, j)),
        jax.ShapeDtypeStruct((slot_count, hidden_units), BF16),
    )(got, joined_weight, joined_weight)


def produce_kernel(hidden, weight, out):
    out[...] = jnp.dot(hidden[...], weight[...], preferred_element_type=F32).astype(BF16)


def produce(hidden, proj_weight, first, columns):
    slot_count, units = hidden.shape
    block = 896
    return call(
        produce_kernel,
        (columns // block,),
        [
            pl.BlockSpec((slot_count, units), lambda j: (0, 0)),
            pl.BlockSpec((units, block), lambda j: (0, first // block + j)),
        ],
        pl.BlockSpec((slot_count, block), lambda j: (0, j)),
        jax.ShapeDtypeStruct((slot_count, columns), BF16),
    )(hidden, proj_weight)


def mix_kernel(mixer, rows, residual, *refs):
    out = refs[-1]
    mixed = lax.dot_general(
        mixer[...], rows[...], (((0,), (0,)), ((), ())), preferred_element_type=F32
    )
    out[...] = (residual[...].astype(F32) + mixed).astype(BF16)


def mix(mixer, rows, residual, first, columns, earlier=None):
    slot_count, tokens = mixer.shape
    block = 896
    in_specs = [
        pl.BlockSpec((slot_count, tokens), lambda j: (0, 0)),
        pl.BlockSpec((slot_count, block), lambda j: (0, j)),
        pl.BlockSpec((tokens, block), lambda j: (0, first // block + j)),
    ]
    operands = [mixer, rows, residual]
    aliases = None
    if earlier is not None:
        in_specs.append(pl.BlockSpec(memory_space=pl.ANY))
        operands.append(earlier)
        aliases = {3: 0}
    return call(
        mix_kernel,
        (columns // block,),
        in_specs,
        pl.BlockSpec((tokens, block), lambda j: (0, first // block + j)),
        jax.ShapeDtypeStruct(residual.shape, BF16),
        aliases=aliases,
    )(*operands)


def gating(tokens, ids, router_section):
    expert_count = router_section.shape[1]
    logits = lax.dot_general(
        router_section, tokens, (((0,), (1,)), ((), ())), preferred_element_type=F32
    )
    hot = ids[:, None, :] == lax.broadcasted_iota(
        jnp.int32, (ids.shape[0], expert_count, ids.shape[1]), 1
    )
    affinity = jax.nn.sigmoid(jnp.sum(jnp.where(hot, logits[None], 0.0), axis=1))
    total = jnp.sum(affinity, axis=0, keepdims=True)
    return affinity, affinity / total, total, hot


def slot_hot(slots, slot_count):
    return slots[:, None, :] == lax.broadcasted_iota(
        jnp.int32, (slots.shape[0], slot_count, slots.shape[1]), 1
    )


def weighted(hot, values):
    return jnp.sum(jnp.where(hot, values[:, None, :], 0.0), axis=0)


def on_device(
    forward_acts,
    forward_ids,
    backward_acts,
    backward_ids,
    upstream_grad,
    gate_up_weight,
    down_weight,
    router_weight,
    mirror_grads,
):
    joined_weight = gate_up_weight[0, 0]
    proj_weight = down_weight[0, 0]
    router_section = router_weight[0]
    tokens_fwd = forward_acts[0]
    tokens_bwd = backward_acts[0]
    upstream = upstream_grad[0]
    ids_fwd = forward_ids[0].T
    ids_bwd = backward_ids[0].T
    mirrored = mirror_grads[0]
    row_count, width = tokens_fwd.shape
    top_count = ids_fwd.shape[0]
    expert_count = router_section.shape[1]
    ranks = lax.axis_size("ep")
    capacity = 3 * row_count * top_count // (2 * ranks)
    slot_count = expert_count * capacity
    shard = width // ranks
    early = width // 2

    sent_bwd, sent_fwd, slots = dispatch(
        ids_bwd, ids_fwd, tokens_bwd, upstream, tokens_fwd, expert_count, capacity
    )
    got_bwd = exchange(sent_bwd)
    (got_bwd, sent_fwd, slots, tokens_fwd, tokens_bwd, upstream, mirrored, router_section) = (
        lax.optimization_barrier(
            (got_bwd, sent_fwd, slots, tokens_fwd, tokens_bwd, upstream, mirrored, router_section)
        )
    )
    got_fwd = exchange(sent_fwd)

    gate_part, up_part, dots = backward_hidden(got_bwd, joined_weight, proj_weight)
    back = exchange(row_gradient(gate_part, up_part, joined_weight, dots))

    hidden = forward_hidden(got_fwd, joined_weight)
    produced_early = shifted(produce(hidden, proj_weight, 0, early), 1)
    produced_late = shifted(produce(hidden, proj_weight, early, width - early), 1)
    residual = shifted(tokens_fwd, 1)
    _, gates_fwd, _, _ = gating(tokens_fwd, ids_fwd, router_section)
    hot_fwd = slot_hot(slots[top_count:], slot_count)
    mixer_fwd = shifted(weighted(hot_fwd, gates_fwd).astype(BF16), 1)
    returned_early = exchange(produced_early)
    next_early = mix(mixer_fwd, returned_early, residual, 0, early)

    affinity, gates_bwd, total, hot_bwd = gating(tokens_bwd, ids_bwd, router_section)
    slots_bwd = slot_hot(slots[:top_count], slot_count)
    gate_rows = back[:, width].astype(F32) + back[:, width + 1].astype(F32)
    gate_grad = jnp.sum(jnp.where(slots_bwd, gate_rows[None, :, None], 0.0), axis=1)
    mean_term = jnp.sum(gates_bwd * gate_grad, axis=0, keepdims=True)
    logit_rows = (gate_grad - mean_term) / total * affinity * (1.0 - affinity)
    logit_grad = weighted(hot_bwd, logit_rows)
    logit_pair = jnp.concatenate(split_two(logit_grad), axis=0)
    router_back = lax.dot_general(
        logit_pair,
        jnp.concatenate([router_section, router_section], axis=1),
        (((0,), (1,)), ((), ())),
        preferred_element_type=F32,
    )
    grad_mix = lax.dot_general(
        weighted(slots_bwd, gates_bwd).astype(BF16),
        back[:, :width],
        (((0,), (0,)), ((), ())),
        preferred_element_type=F32,
    )
    next_grads = shifted((upstream.astype(F32) + grad_mix + router_back).astype(BF16), -1)

    router_pair = jnp.dot(logit_pair, tokens_bwd, preferred_element_type=F32)
    router_part = ((router_pair[:expert_count] + router_pair[expert_count:]) / row_count).astype(
        BF16
    )
    wide = -(-shard // LANES) * LANES
    router_blocks = jnp.pad(
        router_part.reshape(expert_count, ranks, shard).transpose(1, 0, 2),
        ((0, 0), (0, capacity - expert_count), (0, wide - shard)),
    ).reshape(slot_count, wide)
    returned_late = exchange(jnp.concatenate([produced_late, router_blocks], axis=1))
    next_acts = mix(mixer_fwd, returned_late, residual, early, width - early, next_early)

    count = lax.axis_size("pp")
    mirrored = lax.ppermute(mirrored, "pp", [(i, count - 1 - i) for i in range(count)])
    summed = jnp.sum(
        returned_late[:, width - early :]
        .reshape(ranks, capacity, wide)[:, :expert_count, :shard]
        .astype(F32),
        axis=0,
    )
    router_grads = summed.T + mirrored
    return (next_acts[None], next_grads[None], router_grads[None])


def solution(mesh):
    placed = (
        P("pp", "ep", None),
        P("pp", "ep", None),
        P("pp", "ep", None),
        P("pp", "ep", None),
        P("pp", "ep", None),
        P("pp", "ep", None, None),
        P("pp", "ep", None, None),
        P("pp", None, None),
        P("pp", "ep", None),
    )
    return jax.shard_map(
        on_device,
        mesh=mesh,
        in_specs=placed,
        out_specs=(P("pp", "ep", None), P("pp", "ep", None), P("pp", "ep", None)),
        check_vma=False,
    )
```

```python
import functools

import jax
import jax.numpy as jnp
from jax import lax
from jax.experimental import pallas as pl
from jax.experimental.pallas import tpu as pltpu
from jax.sharding import PartitionSpec as P

LANES = 128
BF16 = jnp.bfloat16
F32 = jnp.float32


def shifted(value, steps):
    count = lax.axis_size("pp")
    pairs = [(source, (source + steps) % count) for source in range(count)]
    return lax.ppermute(value, "pp", pairs)


def exchange(value):
    return lax.all_to_all(value, "ep", split_axis=0, concat_axis=0, tiled=True)


def split_two(value):
    high = value.astype(BF16)
    low = (value - high.astype(F32)).astype(BF16)
    return high, low


def call(kernel, grid, in_specs, out_specs, out_shape, scratch=(), aliases=None, limit=48 << 20):
    return pl.pallas_call(
        kernel,
        grid=grid,
        in_specs=in_specs,
        out_specs=out_specs,
        out_shape=out_shape,
        scratch_shapes=scratch,
        input_output_aliases=aliases or {},
        compiler_params=pltpu.CompilerParams(vmem_limit_bytes=limit),
        cost_estimate=pl.CostEstimate(flops=1000, bytes_accessed=1000, transcendentals=0),
    )


def slot_rows(ids, expert_count, capacity):
    top_count, tokens = ids[0].shape
    earlier = (
        lax.broadcasted_iota(jnp.int32, (tokens, tokens), 0)
        < lax.broadcasted_iota(jnp.int32, (tokens, tokens), 1)
    ).astype(F32)
    experts = lax.broadcasted_iota(jnp.int32, (expert_count, tokens), 0)
    named = [batch[k : k + 1] for batch in ids for k in range(top_count)]
    hot = [(experts == row).astype(F32) for row in named]
    counts = jnp.dot(
        jnp.concatenate(hot, axis=0).astype(BF16),
        earlier.astype(BF16),
        preferred_element_type=F32,
    )
    rows = []
    for index, row in enumerate(named):
        before = counts[index * expert_count : (index + 1) * expert_count]
        for other in range(index // top_count * top_count, index):
            before = before + jnp.sum(hot[other], axis=1, keepdims=True)
        place = jnp.sum(before * hot[index], axis=0, keepdims=True)
        rows.append(row * capacity + place.astype(jnp.int32))
    return [rows[first : first + top_count] for first in range(0, len(rows), top_count)]


def picker_of(rows, slot_count):
    tokens = rows[0].shape[1]
    places = lax.broadcasted_iota(jnp.int32, (slot_count, tokens), 0)
    chosen = functools.reduce(jnp.logical_or, [places == row for row in rows])
    return chosen.astype(F32).astype(BF16)


def dispatch_kernel(
    sizes,
    ids_bwd,
    ids_fwd,
    acts_bwd,
    upstream,
    acts_fwd,
    sent_bwd,
    sent_fwd,
    slots,
    loaded,
    built,
    picker,
    arrived,
    left,
):
    expert_count, capacity = sizes
    slot_count = expert_count * capacity
    width = acts_bwd.shape[1]
    loads = [
        pltpu.make_async_copy(source, loaded.at[number], arrived.at[number])
        for number, source in enumerate((acts_fwd, acts_bwd, upstream))
    ]
    for load in loads:
        load.start()
    rows_bwd, rows_fwd = slot_rows([ids_bwd[...], ids_fwd[...]], expert_count, capacity)
    slots[...] = jnp.concatenate(rows_bwd + rows_fwd, axis=0)
    picker[0] = picker_of(rows_fwd, slot_count)
    picker[1] = picker_of(rows_bwd, slot_count)
    loads[0].wait()
    built[...] = jnp.dot(picker[0], loaded[0], preferred_element_type=F32).astype(BF16)
    store = pltpu.make_async_copy(built, sent_fwd, left)
    store.start()
    for number in (1, 2):
        loads[number].wait()
        sent_bwd[:, (number - 1) * width : number * width] = jnp.dot(
            picker[1], loaded[number], preferred_element_type=F32
        ).astype(BF16)
    store.wait()


def dispatch(ids_bwd, ids_fwd, acts_bwd, upstream, acts_fwd, expert_count, capacity):
    tokens, width = acts_bwd.shape
    top_count = ids_bwd.shape[0]
    slot_count = expert_count * capacity
    whole = pl.BlockSpec((top_count, tokens), lambda: (0, 0))
    stays = pl.BlockSpec(memory_space=pl.ANY)
    return call(
        functools.partial(dispatch_kernel, (expert_count, capacity)),
        (),
        [whole, whole, stays, stays, stays],
        [
            pl.BlockSpec(memory_space=pltpu.VMEM),
            stays,
            pl.BlockSpec((2 * top_count, tokens), lambda: (0, 0)),
        ],
        [
            pltpu.VMEM((slot_count, 2 * width), BF16),
            jax.ShapeDtypeStruct((slot_count, width), BF16),
            jax.ShapeDtypeStruct((2 * top_count, tokens), jnp.int32),
        ],
        [
            pltpu.VMEM((3, tokens, width), BF16),
            pltpu.VMEM((slot_count, width), BF16),
            pltpu.VMEM((2, slot_count, tokens), BF16),
            pltpu.SemaphoreType.DMA((3,)),
            pltpu.SemaphoreType.DMA,
        ],
        limit=57982000,
    )(ids_bwd, ids_fwd, acts_bwd, upstream, acts_fwd)


def backward_hidden_kernel(acts, grads, gate_w, up_w, down_w, gate_out, up_out, dots):
    pre_gate = jnp.dot(acts[...], gate_w[...], preferred_element_type=F32)
    pre_up = jnp.dot(acts[...], up_w[...], preferred_element_type=F32)
    hidden_grad = lax.dot_general(
        grads[...], down_w[...], (((1,), (1,)), ((), ())), preferred_element_type=F32
    )
    squash = jax.nn.sigmoid(pre_gate)
    swished = pre_gate * squash
    hidden = (swished * pre_up).astype(BF16).astype(F32)
    gate_out[...] = (
        hidden_grad * pre_up * squash * (1.0 + pre_gate * (1.0 - squash))
    ).astype(BF16)
    up_out[...] = (hidden_grad * swished).astype(BF16)

    @pl.when(pl.program_id(0) == 0)
    def _():
        dots[...] = jnp.zeros_like(dots)

    dots[...] += jnp.sum(hidden * hidden_grad, axis=1, keepdims=True)


def backward_hidden(got, joined_weight, proj_weight):
    slot_count = got.shape[0]
    width = got.shape[1] // 2
    hidden_units = proj_weight.shape[0]
    block = 256
    count = hidden_units // block
    return call(
        backward_hidden_kernel,
        (count,),
        [
            pl.BlockSpec((slot_count, width), lambda j: (0, 0), pipeline_mode=pl.Buffered(1)),
            pl.BlockSpec((slot_count, width), lambda j: (0, 1), pipeline_mode=pl.Buffered(1)),
            pl.BlockSpec((width, block), lambda j: (0, j)),
            pl.BlockSpec((width, block), lambda j: (0, count + j)),
            pl.BlockSpec((block, width), lambda j: (j, 0)),
        ],
        [
            pl.BlockSpec((slot_count, block), lambda j: (0, j)),
            pl.BlockSpec((slot_count, block), lambda j: (0, j)),
            pl.BlockSpec((slot_count, LANES), lambda j: (0, 0)),
        ],
        [
            jax.ShapeDtypeStruct((slot_count, hidden_units), BF16),
            jax.ShapeDtypeStruct((slot_count, hidden_units), BF16),
            jax.ShapeDtypeStruct((slot_count, LANES), F32),
        ],
    )(got, got, joined_weight, joined_weight, proj_weight)


def row_grad_kernel(block, gate_grad, up_grad, weight, dots, out):
    step = pl.program_id(0)
    units = gate_grad.shape[1]
    contract = (((1,), (1,)), ((), ()))
    rows = lax.dot_general(
        gate_grad[...], weight[:, :units], contract, preferred_element_type=F32
    ) + lax.dot_general(up_grad[...], weight[:, units:], contract, preferred_element_type=F32)
    out[:, pl.ds(pl.multiple_of(step * block, block), block)] = rows.astype(BF16)

    @pl.when(step == 0)
    def _():
        high, low = split_two(dots[...])
        lane = lax.broadcasted_iota(jnp.int32, dots.shape, 1)
        extra = jnp.where(lane == 0, high.astype(F32), jnp.where(lane == 1, low.astype(F32), 0.0))
        out[:, out.shape[1] - LANES :] = extra.astype(BF16)


def row_gradient(gate_grad, up_grad, joined_weight, dots):
    slot_count, units = gate_grad.shape
    width = joined_weight.shape[0]
    block = 512
    whole = pl.BlockSpec((slot_count, units), lambda j: (0, 0))
    return call(
        functools.partial(row_grad_kernel, block),
        (width // block,),
        [
            whole,
            whole,
            pl.BlockSpec((block, 2 * units), lambda j: (j, 0)),
            pl.BlockSpec((slot_count, LANES), lambda j: (0, 0)),
        ],
        pl.BlockSpec((slot_count, width + LANES), lambda j: (0, 0)),
        jax.ShapeDtypeStruct((slot_count, width + LANES), BF16),
    )(gate_grad, up_grad, joined_weight, dots)


def forward_hidden_kernel(acts, gate_w, up_w, out):
    pre_gate = jnp.dot(acts[...], gate_w[...], preferred_element_type=F32)
    pre_up = jnp.dot(acts[...], up_w[...], preferred_element_type=F32)
    out[...] = (pre_gate * jax.nn.sigmoid(pre_gate) * pre_up).astype(BF16)


def forward_hidden(got, joined_weight):
    slot_count, width = got.shape
    hidden_units = joined_weight.shape[1] // 2
    block = 256
    count = hidden_units // block
    return call(
        forward_hidden_kernel,
        (count,),
        [
            pl.BlockSpec((slot_count, width), lambda j: (0, 0), pipeline_mode=pl.Buffered(1)),
            pl.BlockSpec((width, block), lambda j: (0, j)),
            pl.BlockSpec((width, block), lambda j: (0, count + j)),
        ],
        pl.BlockSpec((slot_count, block), lambda j: (0, j)),
        jax.ShapeDtypeStruct((slot_count, hidden_units), BF16),
    )(got, joined_weight, joined_weight)


def produce_kernel(hidden, weight, out):
    out[...] = jnp.dot(hidden[...], weight[...], preferred_element_type=F32).astype(BF16)


def produce(hidden, proj_weight, first, columns):
    slot_count, units = hidden.shape
    block = 896
    return call(
        produce_kernel,
        (columns // block,),
        [
            pl.BlockSpec((slot_count, units), lambda j: (0, 0)),
            pl.BlockSpec((units, block), lambda j: (0, first // block + j)),
        ],
        pl.BlockSpec((slot_count, block), lambda j: (0, j)),
        jax.ShapeDtypeStruct((slot_count, columns), BF16),
    )(hidden, proj_weight)


def mix_rows(mixer, rows, residual):
    mixed = lax.dot_general(
        mixer[...], rows[...], (((0,), (0,)), ((), ())), preferred_element_type=F32
    )
    return residual[...].astype(F32) + mixed


def mix_early_kernel(mixer, rows, residual, out):
    out[...] = mix_rows(mixer, rows, residual).astype(BF16)


def mix_early(mixer, rows, residual, block=896):
    slot_count, tokens = mixer.shape
    return call(
        mix_early_kernel,
        (rows.shape[1] // block,),
        [
            pl.BlockSpec((slot_count, tokens), lambda j: (0, 0)),
            pl.BlockSpec((slot_count, block), lambda j: (0, j)),
            pl.BlockSpec((tokens, block), lambda j: (0, j)),
        ],
        pl.BlockSpec((tokens, block), lambda j: (0, j)),
        jax.ShapeDtypeStruct(residual.shape, BF16),
    )(mixer, rows, residual)


def mix_late_kernel(
    capacity, mixer, rows, residual, parts, mirrored, early, grads, out, summed
):
    del early, grads
    out[...] = mix_rows(mixer, rows, residual).astype(BF16)

    @pl.when(pl.program_id(0) == 0)
    def _():
        shape = (mirrored.shape[0], parts.shape[0])
        ahead = lax.broadcasted_iota(jnp.int32, shape, 1) - lax.broadcasted_iota(
            jnp.int32, shape, 0
        )
        chosen = functools.reduce(
            jnp.logical_or, [ahead == place for place in range(0, shape[1], capacity)]
        )
        total = jnp.dot(
            chosen.astype(F32).astype(BF16), parts[...], preferred_element_type=F32
        )
        summed[...] = total[:, : mirrored.shape[1]] + mirrored[...]


def mix_late(mixer, returned, residual, mirrored, early, grads, capacity, wide, block=896):
    slot_count, tokens = mixer.shape
    columns = returned.shape[1] - wide
    first = residual.shape[1] - columns
    stays = pl.BlockSpec(memory_space=pl.ANY)
    whole = pl.BlockSpec(mirrored.shape, lambda j: (0, 0))
    return call(
        functools.partial(mix_late_kernel, capacity),
        (columns // block,),
        [
            pl.BlockSpec((slot_count, tokens), lambda j: (0, 0)),
            pl.BlockSpec((slot_count, block), lambda j: (0, j)),
            pl.BlockSpec((tokens, block), lambda j: (0, first // block + j)),
            pl.BlockSpec((slot_count, wide), lambda j: (0, columns // wide)),
            whole,
            stays,
            stays,
        ],
        [pl.BlockSpec((tokens, block), lambda j: (0, first // block + j)), whole],
        [
            jax.ShapeDtypeStruct(residual.shape, BF16),
            jax.ShapeDtypeStruct(mirrored.shape, F32),
        ],
        aliases={5: 0},
    )(mixer, returned, residual, returned, mirrored, early, grads)


def logit_kernel(extra, slots, ids, affinity, out):
    top_count, tokens = ids.shape
    slot_count = extra.shape[0]
    expert_count = out.shape[0] // 2
    dots = extra[:, 0:1].astype(F32) + extra[:, 1:2].astype(F32)
    places = lax.broadcasted_iota(jnp.int32, (slot_count, tokens), 0)
    experts = lax.broadcasted_iota(jnp.int32, (expert_count, tokens), 0)
    gate_grads = [
        jnp.sum(jnp.where(places == slots[k : k + 1], dots, 0.0), axis=0, keepdims=True)
        for k in range(top_count)
    ]
    rows = [affinity[k : k + 1] for k in range(top_count)]
    total = sum(rows)
    mean_term = sum(row / total * grad for row, grad in zip(rows, gate_grads))
    logit = jnp.zeros((expert_count, tokens), F32)
    for k in range(top_count):
        value = (gate_grads[k] - mean_term) / total * rows[k] * (1.0 - rows[k])
        logit = logit + jnp.where(experts == ids[k : k + 1], value, 0.0)
    out[...] = jnp.concatenate(split_two(logit), axis=0)


def logit_gradient(back, slots, ids, affinity, expert_count):
    slot_count = back.shape[0]
    top_count, tokens = ids.shape
    last = back.shape[1] // LANES - 1
    whole = pl.BlockSpec((top_count, tokens), lambda j: (0, 0))
    return call(
        logit_kernel,
        (1,),
        [
            pl.BlockSpec((slot_count, LANES), lambda j: (0, last)),
            pl.BlockSpec(slots.shape, lambda j: (0, 0)),
            whole,
            whole,
        ],
        pl.BlockSpec((2 * expert_count, tokens), lambda j: (0, 0)),
        jax.ShapeDtypeStruct((2 * expert_count, tokens), BF16),
    )(back, slots, ids, affinity)


def input_grad_kernel(mixer, rows, residual, logit_pair, router, out):
    contract = (((0,), (0,)), ((), ()))
    both = jnp.concatenate([router[...], router[...]], axis=0)
    through = lax.dot_general(logit_pair[...], both, contract, preferred_element_type=F32)
    out[...] = (mix_rows(mixer, rows, residual) + through).astype(BF16)


def input_gradient(mixer, back, residual, logit_pair, router, block=896):
    slot_count, tokens = mixer.shape
    return call(
        input_grad_kernel,
        (residual.shape[1] // block,),
        [
            pl.BlockSpec((slot_count, tokens), lambda j: (0, 0)),
            pl.BlockSpec((slot_count, block), lambda j: (0, j)),
            pl.BlockSpec((tokens, block), lambda j: (0, j)),
            pl.BlockSpec(logit_pair.shape, lambda j: (0, 0)),
            pl.BlockSpec((router.shape[0], block), lambda j: (0, j)),
        ],
        pl.BlockSpec((tokens, block), lambda j: (0, j)),
        jax.ShapeDtypeStruct(residual.shape, BF16),
    )(mixer, back, residual, logit_pair, router)


def settle_kernel(rows, out):
    out[...] = rows[...]


def settled(rows, block=1792):
    tokens, width = rows.shape
    spec = pl.BlockSpec((tokens, block), lambda j: (0, j))
    return call(
        settle_kernel, (width // block,), [spec], spec, jax.ShapeDtypeStruct(rows.shape, BF16)
    )(rows)


def gating(tokens, ids, router_section):
    expert_count = router_section.shape[1]
    logits = lax.dot_general(
        router_section, tokens, (((0,), (1,)), ((), ())), preferred_element_type=F32
    )
    hot = ids[:, None, :] == lax.broadcasted_iota(
        jnp.int32, (ids.shape[0], expert_count, ids.shape[1]), 1
    )
    affinity = jax.nn.sigmoid(jnp.sum(jnp.where(hot, logits[None], 0.0), axis=1))
    total = jnp.sum(affinity, axis=0, keepdims=True)
    return affinity, affinity / total


def slot_hot(slots, slot_count):
    return slots[:, None, :] == lax.broadcasted_iota(
        jnp.int32, (slots.shape[0], slot_count, slots.shape[1]), 1
    )


def weighted(hot, values):
    return jnp.sum(jnp.where(hot, values[:, None, :], 0.0), axis=0)


def on_device(
    forward_acts,
    forward_ids,
    backward_acts,
    backward_ids,
    upstream_grad,
    gate_up_weight,
    down_weight,
    router_weight,
    mirror_grads,
):
    joined_weight = gate_up_weight[0, 0]
    proj_weight = down_weight[0, 0]
    router_section = router_weight[0]
    tokens_fwd = forward_acts[0]
    tokens_bwd = backward_acts[0]
    upstream = upstream_grad[0]
    ids_fwd = forward_ids[0].T
    ids_bwd = backward_ids[0].T
    mirrored = mirror_grads[0]
    row_count, width = tokens_fwd.shape
    top_count = ids_fwd.shape[0]
    expert_count = router_section.shape[1]
    ranks = lax.axis_size("ep")
    capacity = 3 * row_count * top_count // (2 * ranks)
    slot_count = expert_count * capacity
    shard = width // ranks
    early = width // 2

    sent_bwd, sent_fwd, slots = dispatch(
        ids_bwd, ids_fwd, tokens_bwd, upstream, tokens_fwd, expert_count, capacity
    )
    got_bwd = exchange(sent_bwd)
    got_bwd, sent_fwd, slots, mirrored, router_section, here = lax.optimization_barrier(
        (got_bwd, sent_fwd, slots, mirrored, router_section, jnp.ones((), jnp.bool_))
    )
    got_fwd = exchange(sent_fwd)

    gate_part, up_part, dots = backward_hidden(got_bwd, joined_weight, proj_weight)
    back = exchange(row_gradient(gate_part, up_part, joined_weight, dots))

    hidden = forward_hidden(got_fwd, joined_weight)
    produced_early = shifted(produce(hidden, proj_weight, 0, early), 1)
    produced_late = shifted(produce(hidden, proj_weight, early, width - early), 1)
    residual = shifted(jnp.where(here, tokens_fwd, 0), 1)
    _, gates_fwd = gating(tokens_fwd, ids_fwd, router_section)
    hot_fwd = slot_hot(slots[top_count:], slot_count)
    mixer_fwd = shifted(weighted(hot_fwd, gates_fwd).astype(BF16), 1)
    returned_early = exchange(produced_early)
    next_early = mix_early(mixer_fwd, returned_early, residual)

    affinity, gates_bwd = gating(tokens_bwd, ids_bwd, router_section)
    hot_bwd = slot_hot(slots[:top_count], slot_count)
    mixer_bwd = weighted(hot_bwd, gates_bwd).astype(BF16)
    logit_pair = logit_gradient(back, slots, ids_bwd, affinity, expert_count)
    next_grads = settled(
        shifted(input_gradient(mixer_bwd, back, upstream, logit_pair, router_section.T), -1)
    )

    router_pair = jnp.dot(logit_pair, tokens_bwd, preferred_element_type=F32)
    router_part = ((router_pair[:expert_count] + router_pair[expert_count:]) / row_count).astype(
        BF16
    )
    wide = -(-shard // LANES) * LANES
    router_blocks = jnp.pad(
        router_part.reshape(expert_count, ranks, shard).transpose(1, 0, 2),
        ((0, 0), (0, capacity - expert_count), (0, wide - shard)),
    ).reshape(slot_count, wide)
    returned_late = exchange(jnp.concatenate([produced_late, router_blocks], axis=1))
    count = lax.axis_size("pp")
    mirrored = lax.ppermute(mirrored, "pp", [(i, count - 1 - i) for i in range(count)])
    next_acts, router_grads = mix_late(
        mixer_fwd, returned_late, residual, mirrored.T, next_early, next_grads, capacity, wide
    )
    return (next_acts[None], next_grads[None], router_grads.T[None])


def solution(mesh):
    placed = (
        P("pp", "ep", None),
        P("pp", "ep", None),
        P("pp", "ep", None),
        P("pp", "ep", None),
        P("pp", "ep", None),
        P("pp", "ep", None, None),
        P("pp", "ep", None, None),
        P("pp", None, None),
        P("pp", "ep", None),
    )
    return jax.shard_map(
        on_device,
        mesh=mesh,
        in_specs=placed,
        out_specs=(P("pp", "ep", None), P("pp", "ep", None), P("pp", "ep", None)),
        check_vma=False,
    )
```

```python
import functools

import jax
import jax.numpy as jnp
from jax import lax
from jax.experimental import pallas as pl
from jax.experimental.pallas import tpu as pltpu
from jax.sharding import PartitionSpec as P

LANES = 128
BF16 = jnp.bfloat16
F32 = jnp.float32


def shifted(value, steps):
    count = lax.axis_size("pp")
    pairs = [(source, (source + steps) % count) for source in range(count)]
    return lax.ppermute(value, "pp", pairs)


def diagonal(ranks):
    side = int(ranks**0.5)
    return [row * side + (row + turn) % side for turn in range(side) for row in range(side)]


def place_of(rank, ranks):
    side = int(ranks**0.5)
    bits = side.bit_length() - 1
    row, column = rank >> bits, rank & (side - 1)
    return (((column - row) & (side - 1)) << bits) + row


def exchange(value):
    order = diagonal(lax.axis_size("ep"))
    return lax.all_to_all(
        value, "ep", split_axis=0, concat_axis=0, axis_index_groups=[order], tiled=True
    )


def split_two(value):
    high = value.astype(BF16)
    low = (value - high.astype(F32)).astype(BF16)
    return high, low


def call(kernel, grid, in_specs, out_specs, out_shape, scratch=(), aliases=None, limit=48 << 20):
    return pl.pallas_call(
        kernel,
        grid=grid,
        in_specs=in_specs,
        out_specs=out_specs,
        out_shape=out_shape,
        scratch_shapes=scratch,
        input_output_aliases=aliases or {},
        compiler_params=pltpu.CompilerParams(vmem_limit_bytes=limit),
        cost_estimate=pl.CostEstimate(flops=1000, bytes_accessed=1000, transcendentals=0),
    )


def slot_rows(ids, expert_count, capacity):
    top_count, tokens = ids[0].shape
    earlier = (
        lax.broadcasted_iota(jnp.int32, (tokens, tokens), 0)
        < lax.broadcasted_iota(jnp.int32, (tokens, tokens), 1)
    ).astype(F32)
    experts = lax.broadcasted_iota(jnp.int32, (expert_count, tokens), 0)
    named = [batch[k : k + 1] for batch in ids for k in range(top_count)]
    hot = [(experts == row).astype(F32) for row in named]
    counts = jnp.dot(
        jnp.concatenate(hot, axis=0).astype(BF16),
        earlier.astype(BF16),
        preferred_element_type=F32,
    )
    rows = []
    for index, row in enumerate(named):
        before = counts[index * expert_count : (index + 1) * expert_count]
        for other in range(index // top_count * top_count, index):
            before = before + jnp.sum(hot[other], axis=1, keepdims=True)
        place = jnp.sum(before * hot[index], axis=0, keepdims=True)
        rows.append(row * capacity + place.astype(jnp.int32))
    return [rows[first : first + top_count] for first in range(0, len(rows), top_count)]


def picker_of(rows, slot_count):
    tokens = rows[0].shape[1]
    places = lax.broadcasted_iota(jnp.int32, (slot_count, tokens), 0)
    chosen = functools.reduce(jnp.logical_or, [places == row for row in rows])
    return chosen.astype(F32).astype(BF16)


def dispatch_kernel(
    sizes,
    ids_bwd,
    ids_fwd,
    acts_bwd,
    upstream,
    acts_fwd,
    sent_bwd,
    sent_fwd,
    slots,
    loaded,
    built,
    picker,
    arrived,
    left,
):
    expert_count, capacity = sizes
    slot_count = expert_count * capacity
    width = acts_bwd.shape[1]
    loads = [
        pltpu.make_async_copy(source, loaded.at[number], arrived.at[number])
        for number, source in enumerate((acts_fwd, acts_bwd, upstream))
    ]
    for load in loads:
        load.start()
    places = [place_of(ids[...], expert_count) for ids in (ids_bwd, ids_fwd)]
    rows_bwd, rows_fwd = slot_rows(places, expert_count, capacity)
    slots[...] = jnp.concatenate(rows_bwd + rows_fwd, axis=0)
    picker[0] = picker_of(rows_fwd, slot_count)
    picker[1] = picker_of(rows_bwd, slot_count)
    loads[0].wait()
    built[...] = jnp.dot(picker[0], loaded[0], preferred_element_type=F32).astype(BF16)
    store = pltpu.make_async_copy(built, sent_fwd, left)
    store.start()
    for number in (1, 2):
        loads[number].wait()
        sent_bwd[:, (number - 1) * width : number * width] = jnp.dot(
            picker[1], loaded[number], preferred_element_type=F32
        ).astype(BF16)
    store.wait()


def dispatch(ids_bwd, ids_fwd, acts_bwd, upstream, acts_fwd, expert_count, capacity):
    tokens, width = acts_bwd.shape
    top_count = ids_bwd.shape[0]
    slot_count = expert_count * capacity
    whole = pl.BlockSpec((top_count, tokens), lambda: (0, 0))
    stays = pl.BlockSpec(memory_space=pl.ANY)
    return call(
        functools.partial(dispatch_kernel, (expert_count, capacity)),
        (),
        [whole, whole, stays, stays, stays],
        [
            pl.BlockSpec(memory_space=pltpu.VMEM),
            stays,
            pl.BlockSpec((2 * top_count, tokens), lambda: (0, 0)),
        ],
        [
            pltpu.VMEM((slot_count, 2 * width), BF16),
            jax.ShapeDtypeStruct((slot_count, width), BF16),
            jax.ShapeDtypeStruct((2 * top_count, tokens), jnp.int32),
        ],
        [
            pltpu.VMEM((3, tokens, width), BF16),
            pltpu.VMEM((slot_count, width), BF16),
            pltpu.VMEM((2, slot_count, tokens), BF16),
            pltpu.SemaphoreType.DMA((3,)),
            pltpu.SemaphoreType.DMA,
        ],
        limit=57982000,
    )(ids_bwd, ids_fwd, acts_bwd, upstream, acts_fwd)


def backward_hidden_kernel(acts, grads, gate_w, up_w, down_w, gate_out, up_out, dots):
    pre_gate = jnp.dot(acts[...], gate_w[...], preferred_element_type=F32)
    pre_up = jnp.dot(acts[...], up_w[...], preferred_element_type=F32)
    hidden_grad = lax.dot_general(
        grads[...], down_w[...], (((1,), (1,)), ((), ())), preferred_element_type=F32
    )
    squash = jax.nn.sigmoid(pre_gate)
    swished = pre_gate * squash
    hidden = (swished * pre_up).astype(BF16).astype(F32)
    gate_out[...] = (
        hidden_grad * pre_up * squash * (1.0 + pre_gate * (1.0 - squash))
    ).astype(BF16)
    up_out[...] = (hidden_grad * swished).astype(BF16)

    @pl.when(pl.program_id(0) == 0)
    def _():
        dots[...] = jnp.zeros_like(dots)

    dots[...] += jnp.sum(hidden * hidden_grad, axis=1, keepdims=True)


def backward_hidden(got, joined_weight, proj_weight):
    slot_count = got.shape[0]
    width = got.shape[1] // 2
    hidden_units = proj_weight.shape[0]
    block = 256
    count = hidden_units // block
    return call(
        backward_hidden_kernel,
        (count,),
        [
            pl.BlockSpec((slot_count, width), lambda j: (0, 0), pipeline_mode=pl.Buffered(1)),
            pl.BlockSpec((slot_count, width), lambda j: (0, 1), pipeline_mode=pl.Buffered(1)),
            pl.BlockSpec((width, block), lambda j: (0, j)),
            pl.BlockSpec((width, block), lambda j: (0, count + j)),
            pl.BlockSpec((block, width), lambda j: (j, 0)),
        ],
        [
            pl.BlockSpec((slot_count, block), lambda j: (0, j)),
            pl.BlockSpec((slot_count, block), lambda j: (0, j)),
            pl.BlockSpec((slot_count, LANES), lambda j: (0, 0)),
        ],
        [
            jax.ShapeDtypeStruct((slot_count, hidden_units), BF16),
            jax.ShapeDtypeStruct((slot_count, hidden_units), BF16),
            jax.ShapeDtypeStruct((slot_count, LANES), F32),
        ],
    )(got, got, joined_weight, joined_weight, proj_weight)


def row_grad_kernel(block, gate_grad, up_grad, weight, dots, *refs):
    out = refs[-1]
    step = pl.program_id(0)
    units = gate_grad.shape[1]
    contract = (((1,), (1,)), ((), ()))
    rows = lax.dot_general(
        gate_grad[...], weight[:, :units], contract, preferred_element_type=F32
    ) + lax.dot_general(up_grad[...], weight[:, units:], contract, preferred_element_type=F32)
    out[:, pl.ds(pl.multiple_of(step * block, block), block)] = rows.astype(BF16)

    @pl.when(step == 0)
    def _():
        high, low = split_two(dots[...])
        lane = lax.broadcasted_iota(jnp.int32, dots.shape, 1)
        extra = jnp.where(lane == 0, high.astype(F32), jnp.where(lane == 1, low.astype(F32), 0.0))
        out[:, out.shape[1] - LANES :] = extra.astype(BF16)


def row_gradient(gate_grad, up_grad, joined_weight, dots, earlier):
    slot_count, units = gate_grad.shape
    width = joined_weight.shape[0]
    block = 512
    whole = pl.BlockSpec((slot_count, units), lambda j: (0, 0))
    return call(
        functools.partial(row_grad_kernel, block),
        (width // block,),
        [
            whole,
            whole,
            pl.BlockSpec((block, 2 * units), lambda j: (j, 0)),
            pl.BlockSpec((slot_count, LANES), lambda j: (0, 0)),
            pl.BlockSpec(memory_space=pl.ANY),
        ],
        pl.BlockSpec((slot_count, width + LANES), lambda j: (0, 0)),
        jax.ShapeDtypeStruct((slot_count, width + LANES), BF16),
    )(gate_grad, up_grad, joined_weight, dots, earlier)


def forward_hidden_kernel(acts, gate_w, up_w, out):
    pre_gate = jnp.dot(acts[...], gate_w[...], preferred_element_type=F32)
    pre_up = jnp.dot(acts[...], up_w[...], preferred_element_type=F32)
    out[...] = (pre_gate * jax.nn.sigmoid(pre_gate) * pre_up).astype(BF16)


def forward_hidden(got, joined_weight):
    slot_count, width = got.shape
    hidden_units = joined_weight.shape[1] // 2
    block = 256
    count = hidden_units // block
    return call(
        forward_hidden_kernel,
        (count,),
        [
            pl.BlockSpec((slot_count, width), lambda j: (0, 0), pipeline_mode=pl.Buffered(1)),
            pl.BlockSpec((width, block), lambda j: (0, j)),
            pl.BlockSpec((width, block), lambda j: (0, count + j)),
        ],
        pl.BlockSpec((slot_count, block), lambda j: (0, j)),
        jax.ShapeDtypeStruct((slot_count, hidden_units), BF16),
    )(got, joined_weight, joined_weight)


def produce_kernel(hidden, weight, *refs):
    refs[-1][...] = jnp.dot(hidden[...], weight[...], preferred_element_type=F32).astype(BF16)


def produce(hidden, proj_weight, first, columns, block, earlier=()):
    slot_count, units = hidden.shape
    return call(
        produce_kernel,
        (columns // block,),
        [
            pl.BlockSpec((slot_count, units), lambda j: (0, 0)),
            pl.BlockSpec((units, block), lambda j: (0, first // block + j)),
        ]
        + [pl.BlockSpec(memory_space=pl.ANY)] * len(earlier),
        pl.BlockSpec((slot_count, block), lambda j: (0, j)),
        jax.ShapeDtypeStruct((slot_count, columns), BF16),
    )(hidden, proj_weight, *earlier)


def mix_rows(mixer, rows, residual):
    mixed = lax.dot_general(
        mixer[...], rows[...], (((0,), (0,)), ((), ())), preferred_element_type=F32
    )
    return residual[...].astype(F32) + mixed


def mix_early_kernel(mixer, rows, residual, out):
    out[...] = mix_rows(mixer, rows, residual).astype(BF16)


def mix_early(mixer, rows, residual, block):
    slot_count, tokens = mixer.shape
    return call(
        mix_early_kernel,
        (rows.shape[1] // block,),
        [
            pl.BlockSpec((slot_count, tokens), lambda j: (0, 0)),
            pl.BlockSpec((slot_count, block), lambda j: (0, j)),
            pl.BlockSpec((tokens, block), lambda j: (0, j)),
        ],
        pl.BlockSpec((tokens, block), lambda j: (0, j)),
        jax.ShapeDtypeStruct(residual.shape, BF16),
    )(mixer, rows, residual)


def mix_late_kernel(
    capacity, mixer, rows, residual, parts, mirrored, early, grads, out, summed
):
    del early, grads
    out[...] = mix_rows(mixer, rows, residual).astype(BF16)

    @pl.when(pl.program_id(0) == 0)
    def _():
        shape = (mirrored.shape[0], parts.shape[0])
        ahead = lax.broadcasted_iota(jnp.int32, shape, 1) - lax.broadcasted_iota(
            jnp.int32, shape, 0
        )
        chosen = functools.reduce(
            jnp.logical_or, [ahead == place for place in range(0, shape[1], capacity)]
        )
        total = jnp.dot(
            chosen.astype(F32).astype(BF16), parts[...], preferred_element_type=F32
        )
        summed[...] = total[:, : mirrored.shape[1]] + mirrored[...]


def mix_late(mixer, returned, residual, mirrored, early, grads, capacity, wide, block):
    slot_count, tokens = mixer.shape
    columns = returned.shape[1] - wide
    first = residual.shape[1] - columns
    stays = pl.BlockSpec(memory_space=pl.ANY)
    whole = pl.BlockSpec(mirrored.shape, lambda j: (0, 0))
    return call(
        functools.partial(mix_late_kernel, capacity),
        (columns // block,),
        [
            pl.BlockSpec((slot_count, tokens), lambda j: (0, 0)),
            pl.BlockSpec((slot_count, block), lambda j: (0, j)),
            pl.BlockSpec((tokens, block), lambda j: (0, first // block + j)),
            pl.BlockSpec((slot_count, wide), lambda j: (0, columns // wide)),
            whole,
            stays,
            stays,
        ],
        [pl.BlockSpec((tokens, block), lambda j: (0, first // block + j)), whole],
        [
            jax.ShapeDtypeStruct(residual.shape, BF16),
            jax.ShapeDtypeStruct(mirrored.shape, F32),
        ],
        aliases={5: 0},
    )(mixer, returned, residual, returned, mirrored, early, grads)


def logit_kernel(extra, slots, ids, affinity, out):
    top_count, tokens = ids.shape
    slot_count = extra.shape[0]
    expert_count = out.shape[0] // 2
    dots = extra[:, 0:1].astype(F32) + extra[:, 1:2].astype(F32)
    places = lax.broadcasted_iota(jnp.int32, (slot_count, tokens), 0)
    experts = lax.broadcasted_iota(jnp.int32, (expert_count, tokens), 0)
    gate_grads = [
        jnp.sum(jnp.where(places == slots[k : k + 1], dots, 0.0), axis=0, keepdims=True)
        for k in range(top_count)
    ]
    rows = [affinity[k : k + 1] for k in range(top_count)]
    total = sum(rows)
    mean_term = sum(row / total * grad for row, grad in zip(rows, gate_grads))
    logit = jnp.zeros((expert_count, tokens), F32)
    for k in range(top_count):
        value = (gate_grads[k] - mean_term) / total * rows[k] * (1.0 - rows[k])
        logit = logit + jnp.where(experts == ids[k : k + 1], value, 0.0)
    out[...] = jnp.concatenate(split_two(logit), axis=0)


def logit_gradient(back, slots, ids, affinity, expert_count):
    slot_count = back.shape[0]
    top_count, tokens = ids.shape
    last = back.shape[1] // LANES - 1
    whole = pl.BlockSpec((top_count, tokens), lambda j: (0, 0))
    return call(
        logit_kernel,
        (1,),
        [
            pl.BlockSpec((slot_count, LANES), lambda j: (0, last)),
            pl.BlockSpec(slots.shape, lambda j: (0, 0)),
            whole,
            whole,
        ],
        pl.BlockSpec((2 * expert_count, tokens), lambda j: (0, 0)),
        jax.ShapeDtypeStruct((2 * expert_count, tokens), BF16),
    )(back, slots, ids, affinity)


def input_grad_kernel(mixer, rows, residual, logit_pair, router, out):
    contract = (((0,), (0,)), ((), ()))
    both = jnp.concatenate([router[...], router[...]], axis=0)
    through = lax.dot_general(logit_pair[...], both, contract, preferred_element_type=F32)
    out[...] = (mix_rows(mixer, rows, residual) + through).astype(BF16)


def input_gradient(mixer, back, residual, logit_pair, router, block=896):
    slot_count, tokens = mixer.shape
    return call(
        input_grad_kernel,
        (residual.shape[1] // block,),
        [
            pl.BlockSpec((slot_count, tokens), lambda j: (0, 0)),
            pl.BlockSpec((slot_count, block), lambda j: (0, j)),
            pl.BlockSpec((tokens, block), lambda j: (0, j)),
            pl.BlockSpec(logit_pair.shape, lambda j: (0, 0)),
            pl.BlockSpec((router.shape[0], block), lambda j: (0, j)),
        ],
        pl.BlockSpec((tokens, block), lambda j: (0, j)),
        jax.ShapeDtypeStruct(residual.shape, BF16),
    )(mixer, back, residual, logit_pair, router)


def settle_kernel(rows, out):
    out[...] = rows[...]


def settled(rows, block=1792):
    tokens, width = rows.shape
    spec = pl.BlockSpec((tokens, block), lambda j: (0, j))
    return call(
        settle_kernel, (width // block,), [spec], spec, jax.ShapeDtypeStruct(rows.shape, BF16)
    )(rows)


def gating(tokens, ids, router_section):
    expert_count = router_section.shape[1]
    logits = lax.dot_general(
        router_section, tokens, (((0,), (1,)), ((), ())), preferred_element_type=F32
    )
    hot = ids[:, None, :] == lax.broadcasted_iota(
        jnp.int32, (ids.shape[0], expert_count, ids.shape[1]), 1
    )
    affinity = jax.nn.sigmoid(jnp.sum(jnp.where(hot, logits[None], 0.0), axis=1))
    total = jnp.sum(affinity, axis=0, keepdims=True)
    return affinity, affinity / total


def slot_hot(slots, slot_count):
    return slots[:, None, :] == lax.broadcasted_iota(
        jnp.int32, (slots.shape[0], slot_count, slots.shape[1]), 1
    )


def weighted(hot, values):
    return jnp.sum(jnp.where(hot, values[:, None, :], 0.0), axis=0)


def on_device(
    forward_acts,
    forward_ids,
    backward_acts,
    backward_ids,
    upstream_grad,
    gate_up_weight,
    down_weight,
    router_weight,
    mirror_grads,
):
    joined_weight = gate_up_weight[0, 0]
    proj_weight = down_weight[0, 0]
    router_section = router_weight[0]
    tokens_fwd = forward_acts[0]
    tokens_bwd = backward_acts[0]
    upstream = upstream_grad[0]
    ranks = lax.axis_size("ep")
    ids_fwd = forward_ids[0].T
    ids_bwd = backward_ids[0].T
    mirrored = mirror_grads[0]
    row_count, width = tokens_fwd.shape
    top_count = ids_fwd.shape[0]
    expert_count = router_section.shape[1]
    capacity = 3 * row_count * top_count // (2 * ranks)
    slot_count = expert_count * capacity
    shard = width // ranks
    early = 3 * width // 7

    sent_bwd, sent_fwd, slots = dispatch(
        ids_bwd, ids_fwd, tokens_bwd, upstream, tokens_fwd, expert_count, capacity
    )
    got_bwd = exchange(sent_bwd)
    got_bwd, sent_fwd, slots, mirrored, router_section, here = lax.optimization_barrier(
        (got_bwd, sent_fwd, slots, mirrored, router_section, jnp.ones((), jnp.bool_))
    )
    got_fwd = exchange(sent_fwd)

    gate_part, up_part, dots = backward_hidden(got_bwd, joined_weight, proj_weight)
    residual = shifted(jnp.where(here, tokens_fwd, 0), 1)
    back = exchange(row_gradient(gate_part, up_part, joined_weight, dots, residual))

    hidden = forward_hidden(got_fwd, joined_weight)
    rows_early = produce(hidden, proj_weight, 0, early, early // 2)
    rows_late = produce(hidden, proj_weight, early, width - early, early // 3, (rows_early,))
    produced_early = shifted(rows_early, 1)
    produced_late = shifted(rows_late, 1)
    _, gates_fwd = gating(tokens_fwd, ids_fwd, router_section)
    hot_fwd = slot_hot(slots[top_count:], slot_count)
    mixer_fwd = shifted(weighted(hot_fwd, gates_fwd).astype(BF16), 1)
    returned_early = exchange(produced_early)
    next_early = mix_early(mixer_fwd, returned_early, residual, early // 2)

    router_bwd = lax.optimization_barrier((router_section, rows_late))[0]
    affinity, gates_bwd = gating(tokens_bwd, ids_bwd, router_bwd)
    hot_bwd = slot_hot(slots[:top_count], slot_count)
    mixer_bwd = weighted(hot_bwd, gates_bwd).astype(BF16)
    logit_pair = logit_gradient(back, slots, ids_bwd, affinity, expert_count)
    next_grads = settled(
        shifted(input_gradient(mixer_bwd, back, upstream, logit_pair, router_section.T), -1)
    )

    router_pair = jnp.dot(logit_pair, tokens_bwd, preferred_element_type=F32)
    router_part = ((router_pair[:expert_count] + router_pair[expert_count:]) / row_count).astype(
        BF16
    )
    by_rank = router_part.reshape(expert_count, ranks, shard).transpose(1, 0, 2)
    wide = -(-shard // LANES) * LANES
    router_blocks = jnp.pad(
        jnp.stack([by_rank[rank] for rank in diagonal(ranks)]),
        ((0, 0), (0, capacity - expert_count), (0, wide - shard)),
    ).reshape(slot_count, wide)
    returned_late = exchange(jnp.concatenate([produced_late, router_blocks], axis=1))
    count = lax.axis_size("pp")
    mirrored = lax.ppermute(mirrored, "pp", [(i, count - 1 - i) for i in range(count)])
    next_acts, router_grads = mix_late(
        mixer_fwd,
        returned_late,
        residual,
        mirrored.T,
        next_early,
        next_grads,
        capacity,
        wide,
        early // 3,
    )
    return (next_acts[None], next_grads[None], router_grads.T[None])


def solution(mesh):
    placed = (
        P("pp", "ep", None),
        P("pp", "ep", None),
        P("pp", "ep", None),
        P("pp", "ep", None),
        P("pp", "ep", None),
        P("pp", "ep", None, None),
        P("pp", "ep", None, None),
        P("pp", None, None),
        P("pp", "ep", None),
    )
    return jax.shard_map(
        on_device,
        mesh=mesh,
        in_specs=placed,
        out_specs=(P("pp", "ep", None), P("pp", "ep", None), P("pp", "ep", None)),
        check_vma=False,
    )
```

```python
import functools

import jax
import jax.numpy as jnp
from jax import lax
from jax.experimental import pallas as pl
from jax.experimental.pallas import tpu as pltpu
from jax.sharding import PartitionSpec as P

LANES = 128
BF16 = jnp.bfloat16
F32 = jnp.float32


def shifted(value, steps):
    count = lax.axis_size("pp")
    pairs = [(source, (source + steps) % count) for source in range(count)]
    return lax.ppermute(value, "pp", pairs)


def diagonal(ranks):
    side = int(ranks**0.5)
    return [row * side + (row + turn) % side for turn in range(side) for row in range(side)]


def place_of(rank, ranks):
    side = int(ranks**0.5)
    bits = side.bit_length() - 1
    row, column = rank >> bits, rank & (side - 1)
    return (((column - row) & (side - 1)) << bits) + row


def exchange(value):
    order = diagonal(lax.axis_size("ep"))
    return lax.all_to_all(
        value, "ep", split_axis=0, concat_axis=0, axis_index_groups=[order], tiled=True
    )


def split_two(value):
    high = value.astype(BF16)
    low = (value - high.astype(F32)).astype(BF16)
    return high, low


def call(kernel, grid, in_specs, out_specs, out_shape, scratch=(), aliases=None, limit=48 << 20):
    return pl.pallas_call(
        kernel,
        grid=grid,
        in_specs=in_specs,
        out_specs=out_specs,
        out_shape=out_shape,
        scratch_shapes=scratch,
        input_output_aliases=aliases or {},
        compiler_params=pltpu.CompilerParams(vmem_limit_bytes=limit),
        cost_estimate=pl.CostEstimate(flops=1000, bytes_accessed=1000, transcendentals=0),
    )


def slot_rows(ids, expert_count, capacity):
    top_count, tokens = ids[0].shape
    earlier = (
        lax.broadcasted_iota(jnp.int32, (tokens, tokens), 0)
        < lax.broadcasted_iota(jnp.int32, (tokens, tokens), 1)
    ).astype(F32)
    experts = lax.broadcasted_iota(jnp.int32, (expert_count, tokens), 0)
    named = [batch[k : k + 1] for batch in ids for k in range(top_count)]
    hot = [(experts == row).astype(F32) for row in named]
    counts = jnp.dot(
        jnp.concatenate(hot, axis=0).astype(BF16),
        earlier.astype(BF16),
        preferred_element_type=F32,
    )
    rows = []
    for index, row in enumerate(named):
        before = counts[index * expert_count : (index + 1) * expert_count]
        for other in range(index // top_count * top_count, index):
            before = before + jnp.sum(hot[other], axis=1, keepdims=True)
        place = jnp.sum(before * hot[index], axis=0, keepdims=True)
        rows.append(row * capacity + place.astype(jnp.int32))
    return [rows[first : first + top_count] for first in range(0, len(rows), top_count)]


def picker_of(rows, slot_count):
    tokens = rows[0].shape[1]
    places = lax.broadcasted_iota(jnp.int32, (slot_count, tokens), 0)
    chosen = functools.reduce(jnp.logical_or, [places == row for row in rows])
    return chosen.astype(F32).astype(BF16)


def dispatch_kernel(
    sizes,
    ids_bwd,
    ids_fwd,
    acts_bwd,
    upstream,
    acts_fwd,
    sent_bwd,
    sent_fwd,
    slots,
    loaded,
    built,
    picker,
    arrived,
    left,
):
    expert_count, capacity = sizes
    slot_count = expert_count * capacity
    width = acts_bwd.shape[1]
    loads = [
        pltpu.make_async_copy(source, loaded.at[number], arrived.at[number])
        for number, source in enumerate((acts_fwd, acts_bwd, upstream))
    ]
    for load in loads:
        load.start()
    places = [place_of(ids[...], expert_count) for ids in (ids_bwd, ids_fwd)]
    rows_bwd, rows_fwd = slot_rows(places, expert_count, capacity)
    slots[...] = jnp.concatenate(rows_bwd + rows_fwd, axis=0)
    picker[0] = picker_of(rows_fwd, slot_count)
    picker[1] = picker_of(rows_bwd, slot_count)
    loads[0].wait()
    built[...] = jnp.dot(picker[0], loaded[0], preferred_element_type=F32).astype(BF16)
    store = pltpu.make_async_copy(built, sent_fwd, left)
    store.start()
    for number in (1, 2):
        loads[number].wait()
        sent_bwd[:, (number - 1) * width : number * width] = jnp.dot(
            picker[1], loaded[number], preferred_element_type=F32
        ).astype(BF16)
    store.wait()


def dispatch(ids_bwd, ids_fwd, acts_bwd, upstream, acts_fwd, expert_count, capacity):
    tokens, width = acts_bwd.shape
    top_count = ids_bwd.shape[0]
    slot_count = expert_count * capacity
    whole = pl.BlockSpec((top_count, tokens), lambda: (0, 0))
    stays = pl.BlockSpec(memory_space=pl.ANY)
    return call(
        functools.partial(dispatch_kernel, (expert_count, capacity)),
        (),
        [whole, whole, stays, stays, stays],
        [
            pl.BlockSpec(memory_space=pltpu.VMEM),
            stays,
            pl.BlockSpec((2 * top_count, tokens), lambda: (0, 0)),
        ],
        [
            pltpu.VMEM((slot_count, 2 * width), BF16),
            jax.ShapeDtypeStruct((slot_count, width), BF16),
            jax.ShapeDtypeStruct((2 * top_count, tokens), jnp.int32),
        ],
        [
            pltpu.VMEM((3, tokens, width), BF16),
            pltpu.VMEM((slot_count, width), BF16),
            pltpu.VMEM((2, slot_count, tokens), BF16),
            pltpu.SemaphoreType.DMA((3,)),
            pltpu.SemaphoreType.DMA,
        ],
        limit=57982000,
    )(ids_bwd, ids_fwd, acts_bwd, upstream, acts_fwd)


def backward_hidden_kernel(acts, grads, gate_w, up_w, down_w, gate_out, up_out, dots):
    pre_gate = jnp.dot(acts[...], gate_w[...], preferred_element_type=F32)
    pre_up = jnp.dot(acts[...], up_w[...], preferred_element_type=F32)
    hidden_grad = lax.dot_general(
        grads[...], down_w[...], (((1,), (1,)), ((), ())), preferred_element_type=F32
    )
    squash = jax.nn.sigmoid(pre_gate)
    swished = pre_gate * squash
    hidden = (swished * pre_up).astype(BF16).astype(F32)
    gate_out[...] = (
        hidden_grad * pre_up * squash * (1.0 + pre_gate * (1.0 - squash))
    ).astype(BF16)
    up_out[...] = (hidden_grad * swished).astype(BF16)

    @pl.when(pl.program_id(0) == 0)
    def _():
        dots[...] = jnp.zeros_like(dots)

    dots[...] += jnp.sum(hidden * hidden_grad, axis=1, keepdims=True)


def backward_hidden(got, joined_weight, proj_weight):
    slot_count = got.shape[0]
    width = got.shape[1] // 2
    hidden_units = proj_weight.shape[0]
    block = 256
    count = hidden_units // block
    return call(
        backward_hidden_kernel,
        (count,),
        [
            pl.BlockSpec((slot_count, width), lambda j: (0, 0), pipeline_mode=pl.Buffered(1)),
            pl.BlockSpec((slot_count, width), lambda j: (0, 1), pipeline_mode=pl.Buffered(1)),
            pl.BlockSpec((width, block), lambda j: (0, j)),
            pl.BlockSpec((width, block), lambda j: (0, count + j)),
            pl.BlockSpec((block, width), lambda j: (j, 0)),
        ],
        [
            pl.BlockSpec((slot_count, block), lambda j: (0, j)),
            pl.BlockSpec((slot_count, block), lambda j: (0, j)),
            pl.BlockSpec((slot_count, LANES), lambda j: (0, 0)),
        ],
        [
            jax.ShapeDtypeStruct((slot_count, hidden_units), BF16),
            jax.ShapeDtypeStruct((slot_count, hidden_units), BF16),
            jax.ShapeDtypeStruct((slot_count, LANES), F32),
        ],
    )(got, got, joined_weight, joined_weight, proj_weight)


def row_grad_kernel(block, gate_grad, up_grad, weight, dots, *refs):
    out = refs[-1]
    step = pl.program_id(0)
    units = gate_grad.shape[1]
    contract = (((1,), (1,)), ((), ()))
    rows = lax.dot_general(
        gate_grad[...], weight[:, :units], contract, preferred_element_type=F32
    ) + lax.dot_general(up_grad[...], weight[:, units:], contract, preferred_element_type=F32)
    out[:, pl.ds(pl.multiple_of(step * block, block), block)] = rows.astype(BF16)

    @pl.when(step == 0)
    def _():
        high, low = split_two(dots[...])
        lane = lax.broadcasted_iota(jnp.int32, dots.shape, 1)
        extra = jnp.where(lane == 0, high.astype(F32), jnp.where(lane == 1, low.astype(F32), 0.0))
        out[:, out.shape[1] - LANES :] = extra.astype(BF16)


def row_gradient(gate_grad, up_grad, joined_weight, dots, earlier):
    slot_count, units = gate_grad.shape
    width = joined_weight.shape[0]
    block = 512
    whole = pl.BlockSpec((slot_count, units), lambda j: (0, 0))
    return call(
        functools.partial(row_grad_kernel, block),
        (width // block,),
        [
            whole,
            whole,
            pl.BlockSpec((block, 2 * units), lambda j: (j, 0)),
            pl.BlockSpec((slot_count, LANES), lambda j: (0, 0)),
            pl.BlockSpec(memory_space=pl.ANY),
        ],
        pl.BlockSpec((slot_count, width + LANES), lambda j: (0, 0)),
        jax.ShapeDtypeStruct((slot_count, width + LANES), BF16),
    )(gate_grad, up_grad, joined_weight, dots, earlier)


def forward_hidden_kernel(acts, gate_w, up_w, out):
    pre_gate = jnp.dot(acts[...], gate_w[...], preferred_element_type=F32)
    pre_up = jnp.dot(acts[...], up_w[...], preferred_element_type=F32)
    out[...] = (pre_gate * jax.nn.sigmoid(pre_gate) * pre_up).astype(BF16)


def forward_hidden(got, joined_weight):
    slot_count, width = got.shape
    hidden_units = joined_weight.shape[1] // 2
    block = 256
    count = hidden_units // block
    return call(
        forward_hidden_kernel,
        (count,),
        [
            pl.BlockSpec((slot_count, width), lambda j: (0, 0), pipeline_mode=pl.Buffered(1)),
            pl.BlockSpec((width, block), lambda j: (0, j)),
            pl.BlockSpec((width, block), lambda j: (0, count + j)),
        ],
        pl.BlockSpec((slot_count, block), lambda j: (0, j)),
        jax.ShapeDtypeStruct((slot_count, hidden_units), BF16),
    )(got, joined_weight, joined_weight)


def produce_kernel(hidden, weight, *refs):
    refs[-1][...] = jnp.dot(hidden[...], weight[...], preferred_element_type=F32).astype(BF16)


def produce(hidden, proj_weight, first, columns, block, earlier=()):
    slot_count, units = hidden.shape
    return call(
        produce_kernel,
        (columns // block,),
        [
            pl.BlockSpec((slot_count, units), lambda j: (0, 0)),
            pl.BlockSpec((units, block), lambda j: (0, first // block + j)),
        ]
        + [pl.BlockSpec(memory_space=pl.ANY)] * len(earlier),
        pl.BlockSpec((slot_count, block), lambda j: (0, j)),
        jax.ShapeDtypeStruct((slot_count, columns), BF16),
    )(hidden, proj_weight, *earlier)


def mix_rows(mixer, rows, residual):
    mixed = lax.dot_general(
        mixer[...], rows[...], (((0,), (0,)), ((), ())), preferred_element_type=F32
    )
    return residual[...].astype(F32) + mixed


def mix_early_kernel(mixer, rows, residual, out):
    out[...] = mix_rows(mixer, rows, residual).astype(BF16)


def mix_early(mixer, rows, residual, block):
    slot_count, tokens = mixer.shape
    first = residual.shape[1] - rows.shape[1]
    return call(
        mix_early_kernel,
        (rows.shape[1] // block,),
        [
            pl.BlockSpec((slot_count, tokens), lambda j: (0, 0)),
            pl.BlockSpec((slot_count, block), lambda j: (0, j)),
            pl.BlockSpec((tokens, block), lambda j: (0, first // block + j)),
        ],
        pl.BlockSpec((tokens, block), lambda j: (0, first // block + j)),
        jax.ShapeDtypeStruct(residual.shape, BF16),
    )(mixer, rows, residual)


def mix_late_kernel(
    capacity, mixer, rows, residual, parts, mirrored, early, grads, out, summed
):
    del early, grads
    out[...] = mix_rows(mixer, rows, residual).astype(BF16)

    @pl.when(pl.program_id(0) == 0)
    def _():
        shape = (mirrored.shape[0], parts.shape[0])
        ahead = lax.broadcasted_iota(jnp.int32, shape, 1) - lax.broadcasted_iota(
            jnp.int32, shape, 0
        )
        chosen = functools.reduce(
            jnp.logical_or, [ahead == place for place in range(0, shape[1], capacity)]
        )
        total = jnp.dot(
            chosen.astype(F32).astype(BF16), parts[...], preferred_element_type=F32
        )
        summed[...] = total[:, : mirrored.shape[1]] + mirrored[...]


def mix_late(mixer, returned, residual, mirrored, early, grads, capacity, wide, block):
    slot_count, tokens = mixer.shape
    columns = returned.shape[1] - wide
    stays = pl.BlockSpec(memory_space=pl.ANY)
    whole = pl.BlockSpec(mirrored.shape, lambda j: (0, 0))
    return call(
        functools.partial(mix_late_kernel, capacity),
        (columns // block,),
        [
            pl.BlockSpec((slot_count, tokens), lambda j: (0, 0)),
            pl.BlockSpec((slot_count, block), lambda j: (0, j)),
            pl.BlockSpec((tokens, block), lambda j: (0, j)),
            pl.BlockSpec((slot_count, wide), lambda j: (0, columns // wide)),
            whole,
            stays,
            stays,
        ],
        [pl.BlockSpec((tokens, block), lambda j: (0, j)), whole],
        [
            jax.ShapeDtypeStruct(residual.shape, BF16),
            jax.ShapeDtypeStruct(mirrored.shape, F32),
        ],
        aliases={5: 0},
    )(mixer, returned, residual, returned, mirrored, early, grads)


def logit_kernel(extra, slots, ids, affinity, out):
    top_count, tokens = ids.shape
    slot_count = extra.shape[0]
    expert_count = out.shape[0] // 2
    dots = extra[:, 0:1].astype(F32) + extra[:, 1:2].astype(F32)
    places = lax.broadcasted_iota(jnp.int32, (slot_count, tokens), 0)
    experts = lax.broadcasted_iota(jnp.int32, (expert_count, tokens), 0)
    gate_grads = [
        jnp.sum(jnp.where(places == slots[k : k + 1], dots, 0.0), axis=0, keepdims=True)
        for k in range(top_count)
    ]
    rows = [affinity[k : k + 1] for k in range(top_count)]
    total = sum(rows)
    mean_term = sum(row / total * grad for row, grad in zip(rows, gate_grads))
    logit = jnp.zeros((expert_count, tokens), F32)
    for k in range(top_count):
        value = (gate_grads[k] - mean_term) / total * rows[k] * (1.0 - rows[k])
        logit = logit + jnp.where(experts == ids[k : k + 1], value, 0.0)
    out[...] = jnp.concatenate(split_two(logit), axis=0)


def logit_gradient(back, slots, ids, affinity, expert_count):
    slot_count = back.shape[0]
    top_count, tokens = ids.shape
    last = back.shape[1] // LANES - 1
    whole = pl.BlockSpec((top_count, tokens), lambda j: (0, 0))
    return call(
        logit_kernel,
        (1,),
        [
            pl.BlockSpec((slot_count, LANES), lambda j: (0, last)),
            pl.BlockSpec(slots.shape, lambda j: (0, 0)),
            whole,
            whole,
        ],
        pl.BlockSpec((2 * expert_count, tokens), lambda j: (0, 0)),
        jax.ShapeDtypeStruct((2 * expert_count, tokens), BF16),
    )(back, slots, ids, affinity)


def input_grad_kernel(mixer, rows, residual, logit_pair, router, out):
    contract = (((0,), (0,)), ((), ()))
    both = jnp.concatenate([router[...], router[...]], axis=0)
    through = lax.dot_general(logit_pair[...], both, contract, preferred_element_type=F32)
    out[...] = (mix_rows(mixer, rows, residual) + through).astype(BF16)


def input_gradient(mixer, back, residual, logit_pair, router, block=896):
    slot_count, tokens = mixer.shape
    return call(
        input_grad_kernel,
        (residual.shape[1] // block,),
        [
            pl.BlockSpec((slot_count, tokens), lambda j: (0, 0)),
            pl.BlockSpec((slot_count, block), lambda j: (0, j)),
            pl.BlockSpec((tokens, block), lambda j: (0, j)),
            pl.BlockSpec(logit_pair.shape, lambda j: (0, 0)),
            pl.BlockSpec((router.shape[0], block), lambda j: (0, j)),
        ],
        pl.BlockSpec((tokens, block), lambda j: (0, j)),
        jax.ShapeDtypeStruct(residual.shape, BF16),
    )(mixer, back, residual, logit_pair, router)


def settle_kernel(rows, out):
    out[...] = rows[...]


def settled(rows, block=1792):
    tokens, width = rows.shape
    spec = pl.BlockSpec((tokens, block), lambda j: (0, j))
    return call(
        settle_kernel, (width // block,), [spec], spec, jax.ShapeDtypeStruct(rows.shape, BF16)
    )(rows)


def gating(tokens, ids, router_section):
    expert_count = router_section.shape[1]
    logits = lax.dot_general(
        router_section, tokens, (((0,), (1,)), ((), ())), preferred_element_type=F32
    )
    hot = ids[:, None, :] == lax.broadcasted_iota(
        jnp.int32, (ids.shape[0], expert_count, ids.shape[1]), 1
    )
    affinity = jax.nn.sigmoid(jnp.sum(jnp.where(hot, logits[None], 0.0), axis=1))
    total = jnp.sum(affinity, axis=0, keepdims=True)
    return affinity, affinity / total


def slot_hot(slots, slot_count):
    return slots[:, None, :] == lax.broadcasted_iota(
        jnp.int32, (slots.shape[0], slot_count, slots.shape[1]), 1
    )


def weighted(hot, values):
    return jnp.sum(jnp.where(hot, values[:, None, :], 0.0), axis=0)


def on_device(
    forward_acts,
    forward_ids,
    backward_acts,
    backward_ids,
    upstream_grad,
    gate_up_weight,
    down_weight,
    router_weight,
    mirror_grads,
):
    joined_weight = gate_up_weight[0, 0]
    proj_weight = down_weight[0, 0]
    router_section = router_weight[0]
    tokens_fwd = forward_acts[0]
    tokens_bwd = backward_acts[0]
    upstream = upstream_grad[0]
    ranks = lax.axis_size("ep")
    ids_fwd = forward_ids[0].T
    ids_bwd = backward_ids[0].T
    mirrored = mirror_grads[0]
    row_count, width = tokens_fwd.shape
    top_count = ids_fwd.shape[0]
    expert_count = router_section.shape[1]
    capacity = 3 * row_count * top_count // (2 * ranks)
    slot_count = expert_count * capacity
    shard = width // ranks
    early = 3 * width // 7

    sent_bwd, sent_fwd, slots = dispatch(
        ids_bwd, ids_fwd, tokens_bwd, upstream, tokens_fwd, expert_count, capacity
    )
    got_bwd = exchange(sent_bwd)
    got_bwd, sent_fwd, slots, mirrored, router_section, here = lax.optimization_barrier(
        (got_bwd, sent_fwd, slots, mirrored, router_section, jnp.ones((), jnp.bool_))
    )
    got_fwd = exchange(sent_fwd)

    gate_part, up_part, dots = backward_hidden(got_bwd, joined_weight, proj_weight)
    residual = shifted(jnp.where(here, tokens_fwd, 0), 1)
    back = exchange(row_gradient(gate_part, up_part, joined_weight, dots, residual))

    hidden = forward_hidden(got_fwd, joined_weight)
    rows_early = produce(hidden, proj_weight, width - early, early, early // 3)
    rows_late = produce(
        hidden, proj_weight, 0, width - early, (width - early) // 2, (rows_early,)
    )
    produced_early = shifted(rows_early, 1)
    produced_late = shifted(rows_late, 1)
    _, gates_fwd = gating(tokens_fwd, ids_fwd, router_section)
    hot_fwd = slot_hot(slots[top_count:], slot_count)
    mixer_fwd = shifted(weighted(hot_fwd, gates_fwd).astype(BF16), 1)
    returned_early = exchange(produced_early)
    next_early = mix_early(mixer_fwd, returned_early, residual, early // 3)

    router_bwd = lax.optimization_barrier((router_section, rows_late))[0]
    affinity, gates_bwd = gating(tokens_bwd, ids_bwd, router_bwd)
    hot_bwd = slot_hot(slots[:top_count], slot_count)
    mixer_bwd = weighted(hot_bwd, gates_bwd).astype(BF16)
    logit_pair = logit_gradient(back, slots, ids_bwd, affinity, expert_count)
    next_grads = settled(
        shifted(input_gradient(mixer_bwd, back, upstream, logit_pair, router_section.T), -1)
    )

    router_pair = jnp.dot(logit_pair, tokens_bwd, preferred_element_type=F32)
    router_part = ((router_pair[:expert_count] + router_pair[expert_count:]) / row_count).astype(
        BF16
    )
    by_rank = router_part.reshape(expert_count, ranks, shard).transpose(1, 0, 2)
    wide = -(-shard // LANES) * LANES
    router_blocks = jnp.pad(
        jnp.stack([by_rank[rank] for rank in diagonal(ranks)]),
        ((0, 0), (0, capacity - expert_count), (0, wide - shard)),
    ).reshape(slot_count, wide)
    returned_late = exchange(jnp.concatenate([produced_late, router_blocks], axis=1))
    count = lax.axis_size("pp")
    mirrored = lax.ppermute(mirrored, "pp", [(i, count - 1 - i) for i in range(count)])
    next_acts, router_grads = mix_late(
        mixer_fwd,
        returned_late,
        residual,
        mirrored.T,
        next_early,
        next_grads,
        capacity,
        wide,
        (width - early) // 2,
    )
    return (next_acts[None], next_grads[None], router_grads.T[None])


def solution(mesh):
    placed = (
        P("pp", "ep", None),
        P("pp", "ep", None),
        P("pp", "ep", None),
        P("pp", "ep", None),
        P("pp", "ep", None),
        P("pp", "ep", None, None),
        P("pp", "ep", None, None),
        P("pp", None, None),
        P("pp", "ep", None),
    )
    return jax.shard_map(
        on_device,
        mesh=mesh,
        in_specs=placed,
        out_specs=(P("pp", "ep", None), P("pp", "ep", None), P("pp", "ep", None)),
        check_vma=False,
    )
```
